256 devices in a mesh: leaf: 256 (over z, y, x, core).
Axes of the slice: x: 4, y: 4, z: 8, core: 2. Of those that a mesh axis runs over, the one named last changes fastest.
Arguments:
- blocks: float32 [65536, 256], P('leaf'), as said below
- generators: float32 [65536, 256], P('leaf'), as said below
- rhs_blocks: float32 [65536, 128], P('leaf'), may hold values from -24 to 24
Outputs:
- solution: float32 [65536, 128], P('leaf')
- logdet_mean: float32 [], replicated
The draws below stay inside these ranges and needn't reach their ends.
Inputs may be any that keep to these rules, and one draw needn't show every extreme that they name: `blocks`: each block of 256 rows is symmetric positive definite. `generators`: every Schur complement S formed in the merges is symmetric positive definite.
All inputs are finite; a program needn't handle non-finite values.
Results may differ from the reference program's by a relative error of at most 0.0001.
Values sent between devices are 32-bit elements; how exact they have to be, the bound alone decides.
A program may use at most 128 MiB of HBM per device.

```python
import jax
import jax.numpy as jnp
from jax import lax

R = 256
M = 128
LEAVES = 256
UNKNOWNS = 65536


def draw_blocks(key, part):
    key = jax.random.fold_in(key, 11)
    noise_key, diag_key = jax.random.split(key)
    noise = jnp.clip(jax.random.normal(noise_key, (LEAVES, R, R), jnp.float32), -4.0, 4.0)
    diag_values = jax.random.uniform(diag_key, (LEAVES, R), jnp.float32, 7.0, 10.0)
    symmetric = (noise + jnp.swapaxes(noise, 1, 2)) * (0.7071067811865476 / R ** 0.5)
    identity = jnp.eye(R, dtype=jnp.float32)
    result = symmetric * (1.0 - identity) + diag_values[:, :, None] * identity
    return result.reshape(LEAVES * R, R).astype(jnp.float32)


def draw_generators(key, part):
    key = jax.random.fold_in(key, 13)
    values = jnp.clip(jax.random.normal(key, (LEAVES * R, R), jnp.float32), -4.0, 4.0) * 1.5
    return (values * (1.0 / R ** 0.5)).astype(jnp.float32)


def levels(own_key, shape, shards, low, high):
    gain, own = 1.0, jax.random.fold_in(own_key, 6)
    for position, blocks in shards:
        draws = jnp.exp(jax.random.uniform(jax.random.fold_in(own, position), (blocks,), jnp.float32, low / len(shards), high / len(shards)))
        gain = gain * jnp.repeat(draws, shape[position] // blocks).reshape([-1 if axis == position else 1 for axis in range(len(shape))])
    return gain


def normal_values(stream_key, extent, spread, bound, cuts=(), held_as=jnp.bfloat16):
    values = jax.random.normal(stream_key, extent, jnp.float32) * spread
    if len(cuts) > 0:
        values = levels(stream_key, extent, cuts, -0.22, 0.18) * values
    return jnp.clip(values, min=-bound, max=bound).astype(held_as)


def setup_inputs(seed: int = 0) -> dict:
    key_list = jax.random.split(jax.random.key(seed), 4)
    blocks = draw_blocks(jax.random.fold_in(key_list[3], 71), 0)
    generators = draw_generators(jax.random.fold_in(key_list[3], 71), 0)
    rhs_blocks = normal_values(key_list[2], (UNKNOWNS, M), 4.0, 24.0, ((0, 256),), jnp.float32)
    return {"blocks": blocks, "generators": generators, "rhs_blocks": rhs_blocks}


HIGHEST = lax.Precision.HIGHEST

def lower_solve(factor, target):
    return jax.scipy.linalg.solve_triangular(factor, target, lower=True)

def upper_solve(factor, target):
    return jax.scipy.linalg.solve_triangular(factor, target, lower=True, trans='T')

def reference(blocks, generators, rhs_blocks):
    node_block = blocks.reshape(LEAVES, R, R)
    node_gen = generators.reshape(LEAVES, R, R)
    node_rhs = rhs_blocks.reshape(LEAVES, R, M)
    saved_factors = []
    det_sum = jnp.zeros((), jnp.float32)
    height_total = LEAVES.bit_length() - 1
    for height in range(height_total):
        left_block, right_block = (node_block[0::2], node_block[1::2])
        left_gen, right_gen = (node_gen[0::2], node_gen[1::2])
        left_rhs, right_rhs = (node_rhs[0::2], node_rhs[1::2])
        coupling = 0.5 * jnp.einsum('nik,njk->nij', left_gen, right_gen, precision=HIGHEST)
        factor = jnp.linalg.cholesky(left_block)
        reduced = jax.vmap(lower_solve)(factor, coupling)
        carried = jax.vmap(lower_solve)(factor, left_rhs)
        node_block = right_block - jnp.einsum('nki,nkj->nij', reduced, reduced, precision=HIGHEST)
        node_rhs = right_rhs - jnp.einsum('nki,nkj->nij', reduced, carried, precision=HIGHEST)
        node_gen = right_gen
        det_sum = det_sum + 2.0 * jnp.sum(jnp.log(jnp.diagonal(factor, axis1=1, axis2=2)))
        saved_factors.append((factor, reduced, carried))
    root_factor = jnp.linalg.cholesky(node_block[0])
    det_sum = det_sum + 2.0 * jnp.sum(jnp.log(jnp.diagonal(root_factor)))
    solution = upper_solve(root_factor, lower_solve(root_factor, node_rhs[0]))[None]
    for factor, reduced, carried in reversed(saved_factors):
        target = carried - jnp.einsum('nij,njk->nik', reduced, solution, precision=HIGHEST)
        left_value = jax.vmap(upper_solve)(factor, target)
        solution = jnp.stack([left_value, solution], axis=1).reshape(-1, R, M)
    return (solution.reshape(LEAVES * R, M), det_sum / (R * LEAVES))
```

```python
import functools

import jax
import jax.numpy as jnp
from jax import lax
from jax.experimental import pallas as pl
from jax.experimental.pallas import tpu as pltpu
from jax.sharding import PartitionSpec as P

F32 = jnp.float32
B16 = jnp.bfloat16
MESH = pl.DeviceIdType.MESH
G = 8
B = 64

def iota(shape, dim): return lax.broadcasted_iota(jnp.int32, shape, dim)

def group(tiles, pt, j, l, G, zero, put):
    b = tiles[0].shape[0]
    T = tiles[pt]
    call = [jnp.broadcast_to(T[j:, l+t:l+t+1], (b-j, 128)) for t in range(G)]
    c = [x[:G] + zero for x in call]
    D = [X[j:j+G] for X in tiles]
    lane = iota((8, 128), 1); sub = iota((G, 128), 0)
    for q in range(0, G, 4):
        p = lambda s, t: jnp.broadcast_to(c[q+t][q+s:q+s+1], (8, 128))
        a, bb, d = p(0,0), p(0,1), p(1,1)
        e, f, g, h = p(0,2), p(0,3), p(1,2), p(1,3)
        m, n, o = p(2,2), p(2,3), p(3,3)
        det1 = a*d - bb*bb
        i1 = 1.0/det1
        t00, t01 = d*e - bb*g, d*f - bb*h
        t10, t11 = a*g - bb*e, a*h - bb*f
        m2 = m - i1*(e*t00 + g*t10)
        n2 = n - i1*(e*t01 + g*t11)
        o2 = o - i1*(f*t01 + h*t11)
        det2 = m2*o2 - n2*n2
        i2 = 1.0/det2
        u00, u01, u10, u11 = i1*t00, i1*t01, i1*t10, i1*t11
        ia, ib, id_ = i1*a, i1*bb, i1*d
        ja, jb, jd = i2*m2, i2*n2, i2*o2
        put(None, j+q, (det1, det2))
        def apply(X, piv):
            r = [jnp.broadcast_to(X[q+t:q+t+1], (8, 128)) for t in range(4)]
            if piv:
                inp = (lane >= l+q) & (lane < l+q+4)
                r = [jnp.where(inp, jnp.where(lane == l+q+t, 1.0, 0.0), r[t]) for t in range(4)]
            y0, y1 = id_*r[0] - ib*r[1], ia*r[1] - ib*r[0]
            z2 = r[2] - (e*y0 + g*y1)
            z3 = r[3] - (f*y0 + h*y1)
            w2 = jd*z2 - jb*z3
            w3 = ja*z3 - jb*z2
            w0 = (y0 - u01*w3) - u00*w2
            w1 = (y1 - u11*w3) - u10*w2
            W = [w0, w1, w2, w3]
            out = []
            for v in range(G//8):
                xv = X[8*v:8*v+8]
                if piv: xv = jnp.where(inp, 0.0, xv)
                cv = [c[q+t][8*v:8*v+8] for t in range(4)]
                nv = (xv - (cv[2]*w2 + cv[3]*w3)) - (cv[0]*w0 + cv[1]*w1)
                if q//8 == v:
                    for t in range(4): nv = jnp.where(sub[:8] == q%8+t, W[t], nv)
                out.append(nv)
            return jnp.concatenate(out, 0) if len(out) > 1 else out[0]
        nc = list(c)
        for t in range(q+4, G): nc[t] = apply(c[t], False)
        D = [apply(D[i], i == pt) for i in range(len(tiles))]
        c = nc
    out = []
    inpG = (lane >= l) & (lane < l+G)
    for ti, X in enumerate(tiles):
        put(ti, j, D[ti])
        vs = [X[:j+G]]
        if j+G < b:
            R = [jnp.broadcast_to(D[ti][t:t+1], (8, 128)) for t in range(G)]
            for v in range(G//8, (b-j)//8):
                xv = X[j+8*v:j+8*v+8]
                if ti == pt: xv = jnp.where(inpG, 0.0, xv)
                acc = [None]*4
                for t in range(G):
                    pr = call[t][8*v:8*v+8]*R[t]
                    k = t % 4
                    acc[k] = pr if acc[k] is None else acc[k] + pr
                vs.append(xv - ((acc[0]+acc[1]) + (acc[2]+acc[3])))
        out.append(jnp.concatenate(vs, 0) if len(vs) > 1 else vs[0])
    return out

def split(x):
    hi = x.astype(B16); return hi, (x - hi.astype(F32)).astype(B16)
def mm3(a, b, dn):
    (ah, al), (bh, bl) = a, b
    dg = lambda u, v: lax.dot_general(u, v, dn, preferred_element_type=F32)
    return dg(ah, bh) + (dg(ah, bl) + dg(al, bh))
NN = (((1,), (0,)), ((), ()))
TN = (((0,), (0,)), ((), ()))
NT = (((1,), (1,)), ((), ()))


def copy_to(src, dst, send, recv, device):
    return pltpu.make_async_remote_copy(
        src_ref=src, dst_ref=dst, send_sem=send, recv_sem=recv, device_id=(device,), device_id_type=MESH
    )


def kernel(n, s_in, w_in, g_in, x_out, ld_out, S, W, Wp, Up, up, Uo, uo, CG, Rs, ZC, RC, E, Y, Yp, det, zero_ref,
           sw, rw, sU, rU, su, ru, sx, rx):
    height = n.bit_length() - 1
    me = lax.axis_index("leaf")
    k1 = me + 1
    has = [k1 % (2 << l) == 0 for l in range(height)]
    child = [me - (1 << l) for l in range(height)]
    depth = sum(h.astype(jnp.int32) for h in has)
    parent = me + 1 + sum(jnp.where(has[l], 1 << l, 0) for l in range(height))
    inner = me != n - 1
    R, M = g_in.shape
    nk = R // B

    barrier = pltpu.get_barrier_semaphore()
    for l in range(height):
        @pl.when(has[l])
        def _():
            pl.semaphore_signal(barrier, inc=1, device_id=(child[l],), device_id_type=MESH)
    @pl.when(inner)
    def _():
        pl.semaphore_signal(barrier, inc=1, device_id=(parent,), device_id_type=MESH)
    pl.semaphore_wait(barrier, depth + inner.astype(jnp.int32))

    s0 = s_in[...]
    eye = iota((R, R), 0) == iota((R, R), 1)
    diag = jnp.where(eye, s0, 0.0)
    drow = jnp.sum(diag, axis=0, keepdims=True)
    scol = lax.rsqrt(jnp.sum(diag, axis=1, keepdims=True))
    W[...] = w_in[...] * scol
    for l in range(height):
        @pl.when(has[l])
        def _():
            copy_to(W, Wp, sw.at[l], rw, child[l]).start()
    S[...] = s0 * scol * lax.rsqrt(drow)
    CG[:, R:] = g_in[...] * scol
    zero_ref[...] = jnp.zeros_like(zero_ref)
    own = jnp.sum(jnp.log(drow), axis=1, keepdims=True)

    @pl.when(inner)
    def _():
        copy_to(W, Wp, sw.at[0], rw, parent).wait_recv()
        CG[:, :R] = 0.5 * mm3(split(W[...]), split(Wp[...]), NT)
    @pl.when(jnp.logical_not(inner))
    def _():
        CG[:, :R] = jnp.zeros((R, R), F32)

    for l in range(height):
        @pl.when(has[l])
        def _():
            copy_to(Uo, Up.at[l], sU, rU.at[l], parent).wait_recv()
            S[...] += Up[l]
            copy_to(uo, up.at[l], su, ru.at[l], parent).wait_recv()
            CG[:, R:] += up[l, :R]

    zero = zero_ref[...]
    row = iota((B, 128), 0)
    lane = iota((B, 128), 1)
    for k in range(nk):
        pt, lb = (B * k) // 128, (B * k) % 128
        rows = slice(B * k, B * k + B)
        t0 = pt
        tiles = [S[rows, 128 * t:128 * t + 128] for t in range(t0, R // 128)]
        def put(ti, j, val):
            if ti is None:
                r0 = (B * k + j) // 2
                det[r0:r0 + 1, :] = val[0][0:1]
                det[r0 + 1:r0 + 2, :] = val[1][0:1]
            else:
                Rs[B * k + j:B * k + j + G, 128 * (t0 + ti):128 * (t0 + ti) + 128] = val
        for j in range(0, B, G):
            tiles = group(tiles, 0, j, lb + j, G, zero, put)
        Z = jnp.concatenate(tiles, 1) if len(tiles) > 1 else tiles[0]
        S[rows, 128 * t0:] = Z
        lo = B * (k + 1)
        zs = split(Z)
        if k < nk - 1:
            upd = mm3(zs, split(Rs[rows, 128 * t0:]), TN)
            S[lo:, 128 * t0:] -= upd[lo - 128 * t0:]
        rel = lane - lb
        inside = (rel >= 0) & (rel < B)
        Lk = jnp.where(inside & (rel < G * (row // G)), tiles[0], jnp.where(rel == row, 1.0, 0.0))
        DLk = jnp.where(inside & (rel < G * (row // G) + G), Rs[rows, 128 * t0:128 * t0 + 128], 0.0)
        S[rows, 128 * t0:128 * t0 + 128] = Lk
        both = mm3(split(jnp.concatenate([Lk, DLk], 0)), split(CG[128 * pt:128 * pt + 128, :]), NN)
        ZC[rows, :] = both[:B, :R]
        RC[rows, :] = both[B:]
        if k < nk - 1:
            upd = mm3(zs, split(RC[rows, :]), TN)
            CG[lo:, :] -= upd[lo - 128 * t0:]
        if k == nk - 2:
            upd = mm3(split(ZC[:lo, :]), split(RC[:lo, :]), TN)
            Uo[...] = -upd[:, :R]
            uo[:R, :] = -upd[:, R:]
    rows = slice(R - B, R)
    upd = mm3(split(ZC[rows, :]), split(RC[rows, :]), TN)
    Uo[...] -= upd[:, :R]
    @pl.when(inner)
    def _():
        for l in range(height):
            @pl.when(depth == l)
            def _():
                copy_to(Uo, Up.at[l], sU, rU.at[l], parent).start()
    uo[:R, :] -= upd[:, R:]
    own = own + jnp.sum(jnp.log(det[...]), axis=0, keepdims=True)
    ld_out[...] = jnp.broadcast_to(own, (8, 128))
    for l in range(height):
        @pl.when(has[l])
        def _():
            ld_out[...] += up[l, R:]
    uo[R:, :] = ld_out[...]
    @pl.when(inner)
    def _():
        for l in range(height):
            @pl.when(depth == l)
            def _():
                copy_to(uo, up.at[l], su, ru.at[l], parent).start()

    for k in reversed(range(nk)):
        pt = (B * k) // 128
        rows = slice(B * k, B * k + B)
        hi = B * (k + 1)
        rhs = RC[rows, :]
        if k < nk - 1:
            base = 128 * pt
            r = Rs[rows, base:]
            r = jnp.where(iota(r.shape, 1) >= hi - base, r, 0.0)
            e = E[base:, :]
            e = jnp.where(iota(e.shape, 0) >= hi - base, e, 0.0)
            rhs = rhs - mm3(split(r), split(e), NN)
        sol = mm3(split(S[rows, 128 * pt:128 * pt + 128]), split(rhs), TN)
        E[rows, :] = sol[B * k - 128 * pt:B * k - 128 * pt + B]

    @pl.when(inner)
    def _():
        copy_to(Y, Yp, sx.at[0], rx, parent).wait_recv()
        Y[:R, :] = E[:, R:] - mm3(split(E[:, :R]), split(Yp[:R, :]), NN)
        Y[R:, :] = Yp[R:, :]
    @pl.when(jnp.logical_not(inner))
    def _():
        Y[:R, :] = E[:, R:]
        Y[R:, :] = ld_out[...] / (R * n)
    for l in reversed(range(height)):
        @pl.when(has[l])
        def _():
            copy_to(Y, Yp, sx.at[l], rx, child[l]).start()
    x_out[...] = Y[:R, :] * scol
    ld_out[...] = Y[R:, :]
    for l in range(height):
        @pl.when(has[l])
        def _():
            copy_to(W, Wp, sw.at[l], rw, child[l]).wait_send()
            copy_to(Y, Yp, sx.at[l], rx, child[l]).wait_send()
    @pl.when(inner)
    def _():
        copy_to(Uo, Up.at[0], sU, rU.at[0], parent).wait_send()
        copy_to(uo, up.at[0], su, ru.at[0], parent).wait_send()


def local(n, blocks, generators, rhs_blocks):
    R, M = rhs_blocks.shape
    height = n.bit_length() - 1
    dma = pltpu.SemaphoreType.DMA
    vm = lambda *s: pltpu.VMEM(s, F32)
    x, ld = pl.pallas_call(
        functools.partial(kernel, n),
        out_shape=(jax.ShapeDtypeStruct((R, M), F32), jax.ShapeDtypeStruct((8, 128), F32)),
        in_specs=[pl.BlockSpec(memory_space=pltpu.VMEM)] * 3,
        out_specs=[pl.BlockSpec(memory_space=pltpu.VMEM)] * 2,
        scratch_shapes=[
            vm(R, R), vm(R, R), vm(R, R), vm(height, R, R), vm(height, R + 8, M), vm(R, R), vm(R + 8, M),
            vm(R, R + M), vm(R, R), vm(R, R), vm(R, R + M), vm(R, R + M), vm(R + 8, M), vm(R + 8, M), vm(R // 2, 128), vm(G, 128),
            dma((height,)), dma, dma, dma((height,)), dma, dma((height,)), dma((height,)), dma,
        ],
        compiler_params=pltpu.CompilerParams(
            collective_id=0, has_side_effects=True, vmem_limit_bytes=40 * 1024 * 1024
        ),
        name="ulv",
    )(blocks, generators, rhs_blocks)
    return x, ld[0, 0]


def solution(mesh):
    n = mesh.shape["leaf"]
    return jax.shard_map(
        functools.partial(local, n),
        mesh=mesh,
        in_specs=(P("leaf", None), P("leaf", None), P("leaf", None)),
        out_specs=(P("leaf", None), P()),
        check_vma=False,
    )
```

```python
import functools

import jax
import jax.numpy as jnp
from jax import lax
from jax.experimental import pallas as pl
from jax.experimental.pallas import tpu as pltpu
from jax.sharding import PartitionSpec as P

F32 = jnp.float32
B16 = jnp.bfloat16
MESH = pl.DeviceIdType.MESH
G = 8
B = 64
NC = 2

def iota(shape, dim): return lax.broadcasted_iota(jnp.int32, shape, dim)

def group(tiles, pt, j, l, G, zero, put):
    b = tiles[0].shape[0]
    T = tiles[pt]
    call = [jnp.broadcast_to(T[j:, l+t:l+t+1], (b-j, 128)) for t in range(G)]
    c = [x[:G] + zero for x in call]
    D = [X[j:j+G] for X in tiles]
    lane = iota((8, 128), 1); sub = iota((G, 128), 0)
    for q in range(0, G, 4):
        p = lambda s, t: jnp.broadcast_to(c[q+t][q+s:q+s+1], (8, 128))
        a, bb, d = p(0,0), p(0,1), p(1,1)
        e, f, g, h = p(0,2), p(0,3), p(1,2), p(1,3)
        m, n, o = p(2,2), p(2,3), p(3,3)
        det1 = a*d - bb*bb
        i1 = 1.0/det1
        t00, t01 = d*e - bb*g, d*f - bb*h
        t10, t11 = a*g - bb*e, a*h - bb*f
        m2 = m - i1*(e*t00 + g*t10)
        n2 = n - i1*(e*t01 + g*t11)
        o2 = o - i1*(f*t01 + h*t11)
        det2 = m2*o2 - n2*n2
        i2 = 1.0/det2
        u00, u01, u10, u11 = i1*t00, i1*t01, i1*t10, i1*t11
        ia, ib, id_ = i1*a, i1*bb, i1*d
        ja, jb, jd = i2*m2, i2*n2, i2*o2
        put(None, j+q, (det1, det2))
        def apply(X, piv):
            r = [jnp.broadcast_to(X[q+t:q+t+1], (8, 128)) for t in range(4)]
            if piv:
                inp = (lane >= l+q) & (lane < l+q+4)
                r = [jnp.where(inp, jnp.where(lane == l+q+t, 1.0, 0.0), r[t]) for t in range(4)]
            y0, y1 = id_*r[0] - ib*r[1], ia*r[1] - ib*r[0]
            z2 = r[2] - (e*y0 + g*y1)
            z3 = r[3] - (f*y0 + h*y1)
            w2 = jd*z2 - jb*z3
            w3 = ja*z3 - jb*z2
            w0 = (y0 - u01*w3) - u00*w2
            w1 = (y1 - u11*w3) - u10*w2
            W = [w0, w1, w2, w3]
            out = []
            for v in range(G//8):
                xv = X[8*v:8*v+8]
                if piv: xv = jnp.where(inp, 0.0, xv)
                cv = [c[q+t][8*v:8*v+8] for t in range(4)]
                nv = (xv - (cv[2]*w2 + cv[3]*w3)) - (cv[0]*w0 + cv[1]*w1)
                if q//8 == v:
                    for t in range(4): nv = jnp.where(sub[:8] == q%8+t, W[t], nv)
                out.append(nv)
            return jnp.concatenate(out, 0) if len(out) > 1 else out[0]
        nc = list(c)
        for t in range(q+4, G): nc[t] = apply(c[t], False)
        D = [apply(D[i], i == pt) for i in range(len(tiles))]
        c = nc
    out = []
    inpG = (lane >= l) & (lane < l+G)
    for ti, X in enumerate(tiles):
        put(ti, j, D[ti])
        vs = [X[:j+G]]
        if j+G < b:
            R = [jnp.broadcast_to(D[ti][t:t+1], (8, 128)) for t in range(G)]
            for v in range(G//8, (b-j)//8):
                xv = X[j+8*v:j+8*v+8]
                if ti == pt: xv = jnp.where(inpG, 0.0, xv)
                acc = [None]*4
                for t in range(G):
                    pr = call[t][8*v:8*v+8]*R[t]
                    k = t % 4
                    acc[k] = pr if acc[k] is None else acc[k] + pr
                vs.append(xv - ((acc[0]+acc[1]) + (acc[2]+acc[3])))
        out.append(jnp.concatenate(vs, 0) if len(vs) > 1 else vs[0])
    return out

def split(x):
    hi = x.astype(B16); return hi, (x - hi.astype(F32)).astype(B16)
def mm3(a, b, dn):
    (ah, al), (bh, bl) = a, b
    dg = lambda u, v: lax.dot_general(u, v, dn, preferred_element_type=F32)
    return dg(ah, bh) + (dg(ah, bl) + dg(al, bh))
NN = (((1,), (0,)), ((), ()))
TN = (((0,), (0,)), ((), ()))
NT = (((1,), (1,)), ((), ()))


def copy_to(src, dst, send, recv, device):
    return pltpu.make_async_remote_copy(
        src_ref=src, dst_ref=dst, send_sem=send, recv_sem=recv, device_id=(device,), device_id_type=MESH
    )


def kernel(n, s_hbm, w_hbm, g_hbm, x_out, ld_out, s_in, w_in, g_in, S, Sx, W, WB, SB, GB, GX, Uo, CG, Rs, F, ZC, RC, E, Eh, El, DT, Y,
           det, ld_acc, zero_ref, sin, sw, rw, sS, rS, sg, rg, sx, rx):
    height = n.bit_length() - 1
    me = lax.axis_index("leaf")
    R, M = g_hbm.shape
    nk = R // B
    H = R // 2
    C = M // NC
    s_parts = [(slice(0, H), slice(0, R)), (slice(H, R), slice(H, R))]
    y_parts = [slice(C * c, C * c + C + (8 if c == NC - 1 else 0)) for c in range(NC)]
    left = [me % (2 << l) == 0 for l in range(height)]
    gives = [(me + 1) % (2 << l) == 0 for l in range(height)]
    rest = me != 0
    count = lambda flags: sum(f.astype(jnp.int32) for f in flags)
    span = 1 + sum(jnp.where(left[l], 1 << l, 0) for l in range(height))
    top = me - span

    loads = [pltpu.make_async_copy(a, b, sin.at[i]) for i, (a, b) in enumerate([(s_hbm, s_in), (w_hbm, w_in), (g_hbm, g_in)])]
    for load in loads:
        load.start()
    barrier = pltpu.get_barrier_semaphore()
    for l in range(height):
        @pl.when(left[l])
        def _():
            pl.semaphore_signal(barrier, inc=1, device_id=(me + (2 << l) - 1,), device_id_type=MESH)
            pl.semaphore_signal(barrier, inc=1, device_id=(me + (1 << l),), device_id_type=MESH)
    @pl.when(rest)
    def _():
        pl.semaphore_signal(barrier, inc=1, device_id=(top,), device_id_type=MESH)

    loads[0].wait()
    s0 = s_in[...]
    eye = iota((R, R), 0) == iota((R, R), 1)
    diag = jnp.where(eye, s0, 0.0)
    drow = jnp.sum(diag, axis=0, keepdims=True)
    scol = lax.rsqrt(jnp.sum(diag, axis=1, keepdims=True))
    srow = lax.rsqrt(drow)
    S[...] = s0 * scol * srow
    loads[1].wait()
    W[...] = w_in[...] * scol
    loads[2].wait()
    CG[:, R:] = g_in[...] * scol
    zero_ref[...] = jnp.zeros_like(zero_ref)
    WB[height] = jnp.zeros((R, R), F32)
    ld_acc[...] = jnp.broadcast_to(jnp.sum(jnp.log(drow), axis=1, keepdims=True), (8, 128))
    pl.semaphore_wait(barrier, count(left) + count(gives) + rest.astype(jnp.int32))

    def send_state(level, target):
        for i, part in enumerate(s_parts):
            Sx[part] = S[part]
            copy_to(Sx.at[part], SB.at[(level,) + part], sS.at[i], rS.at[level, i], target).start()

    def send_rhs(level, target):
        GX[:R, :] = CG[:, R:]
        GX[R:, :] = ld_acc[...]
        copy_to(GX, GB.at[level], sg, rg.at[level], target).start()

    @pl.when(me % 2 != 0)
    def _():
        send_state(0, me - 1)
    for l in range(height):
        @pl.when(gives[l])
        def _():
            copy_to(W, WB.at[l], sw.at[l], rw.at[l], me + 1 - (2 << l)).start()
    @pl.when(me % 2 != 0)
    def _():
        send_rhs(0, me - 1)

    row = iota((B, 128), 0)
    lane = iota((B, 128), 1)

    def level(it, st):
        last = it == height

        @pl.when(me % (2 * st) == 0)
        def _():
            @pl.when(jnp.logical_not(last))
            def _():
                copy_to(W, WB.at[it], sw.at[0], rw.at[it], me).wait_recv()
            zero = zero_ref[...]
            for k in range(nk):
                lb = (B * k) % 128
                base = B * k - lb
                lo = B * (k + 1)
                rows, pair = slice(B * k, lo), slice(base, base + 128)
                tiles = [S[rows, t:t + 128] for t in range(base, R, 128)]
                def put(ti, j, val):
                    if ti is None:
                        r0 = (rows.start + j) // 2
                        det[r0:r0 + 1, :] = val[0][0:1]
                        det[r0 + 1:r0 + 2, :] = val[1][0:1]
                    else:
                        Rs[rows.start + j:rows.start + j + G, base + 128 * ti:base + 128 * ti + 128] = val
                for j in range(0, B, G):
                    tiles = group(tiles, 0, j, lb + j, G, zero, put)
                Z = jnp.concatenate(tiles, 1) if len(tiles) > 1 else tiles[0]
                zs = split(Z)
                if k < nk - 1:
                    upd = mm3(zs, split(Rs[rows, base:]), TN)
                    S[lo:, base:] -= upd[lo - base:]
                if k == 0:
                    wb = WB[it]
                    CG[:, :R] = 0.5 * mm3(split(W[...]), split(wb), NT)
                rel = lane - lb
                inside = (rel >= 0) & (rel < B)
                Lk = jnp.where(inside & (rel < G * (row // G)), tiles[0], jnp.where(rel == row, 1.0, 0.0))
                DLk = jnp.where(inside & (rel < G * (row // G) + G), Rs[rows, pair], 0.0)
                both = mm3(split(jnp.concatenate([Lk, DLk], 0)), split(CG[pair, :]), NN)
                ZC[rows, :] = both[:B, :R]
                rc = both[B:]
                RC[rows, :] = rc
                ls = split(Lk)
                if k < nk - 1:
                    upd = mm3(zs, split(rc), TN)
                    CG[lo:, :] -= upd[lo - base:]
                    rs = Rs[rows, base:]
                    rs = jnp.where(iota(rs.shape, 1) >= lo - base, rs, 0.0)
                    ft = mm3(ls, split(rs), TN)[lb:lb + B]
                    F[rows, base:] = ft
                    ek = mm3(ls, split(rc), TN)[lb:lb + B]
                    E[rows, :] = ek
                    if k:
                        f = jnp.where((iota((B * k, 128), 1) >= lb) & (iota((B * k, 128), 1) < lb + B), F[:B * k, pair], 0.0)
                        gap = jnp.zeros_like
                        pad = (lambda v: jnp.concatenate([v, gap(v)], 0)) if lb == 0 else (lambda v: jnp.concatenate([gap(v), v], 0))
                        fs = split(f)
                        E[:B * k, :] -= mm3(fs, split(pad(ek)), NN)
                        F[:B * k, base:] -= mm3(fs, split(pad(ft)), NN)
                if k == nk - 2:
                    zc, rr = split(ZC[:lo, :]), split(RC[:lo, :])
                    Uo[:H, :] = mm3([a[:, :H] for a in zc], rr, TN)
                    Uo[H:, H:] = mm3([a[:, H:] for a in zc], [a[:, H:] for a in rr], TN)

            ek = mm3(ls, split(rc), TN)[lb:]
            E[rows, :] = ek
            f = jnp.where(iota((R - B, 128), 1) >= lb, F[:R - B, pair], 0.0)
            E[:R - B, :] -= mm3(split(f), split(jnp.concatenate([jnp.zeros_like(ek), ek], 0)), NN)
            et = E[...]
            Eh[it], El[it] = split(et[:, :R].T)
            DT[it] = et[:, R:].T
            ld_acc[...] += jnp.broadcast_to(jnp.sum(jnp.log(det[...]), axis=0, keepdims=True), (8, 128))

            @pl.when(jnp.logical_not(last))
            def _():
                for i, part in enumerate(s_parts):
                    copy_to(Sx.at[part], SB.at[(it,) + part], sS.at[i], rS.at[it, i], me).wait_recv()
                zc, rr = split(ZC[rows, :]), split(RC[rows, :])
                ua = Uo[:H, :] + mm3([a[:, :H] for a in zc], rr, TN)
                ub = Uo[H:, H:] + mm3([a[:, H:] for a in zc], [a[:, H:] for a in rr], TN)
                S[:H, :] = SB[it, :H, :] - ua[:, :R]
                S[H:, H:] = SB[it, H:, H:] - ub[:, :H]
                turn = me % (4 * st) != 0
                @pl.when(turn)
                def _():
                    send_state(it + 1, top)
                copy_to(GX, GB.at[it], sg, rg.at[it], me).wait_recv()
                CG[:H, R:] = GB[it, :H] - ua[:, R:]
                CG[H:, R:] = GB[it, H:R] - ub[:, H:]
                ld_acc[...] += GB[it, R:]
                @pl.when(turn)
                def _():
                    send_rhs(it + 1, top)
                W[...] = WB[it]
        return st * 2

    lax.fori_loop(0, height + 1, level, jnp.int32(1))

    @pl.when(jnp.logical_not(rest))
    def _():
        Y[height, :M, :] = DT[height]
        Y[height, M:, :] = jnp.broadcast_to(ld_acc[0:1, 0:1] / (R * n), (8, R))

    def down(i, st):
        it = height - 1 - i

        @pl.when(me % (2 * st) == 0)
        def _():
            for c in range(NC):
                @pl.when(rest & (span == 2 * st))
                def _():
                    copy_to(Y.at[it + 1, y_parts[c]], Y.at[it + 1, y_parts[c]], sx.at[it, c], rx.at[c], me).wait_recv()
                copy_to(Y.at[it + 1, y_parts[c]], Y.at[it, y_parts[c]], sx.at[it, c], rx.at[c], me + st).start()
            for c in range(NC):
                r = slice(C * c, C * c + C)
                ah, al = split(Y[it + 1, r, :])
                dg = lambda a, b: jnp.dot(a, b, preferred_element_type=F32)
                Y[it, r, :] = DT[it, r, :] - (dg(ah, Eh[it]) + (dg(al, Eh[it]) + dg(ah, El[it])))
            Y[it, M:, :] = Y[it + 1, M:, :]
        return st // 2

    lax.fori_loop(0, height, down, jnp.int32(n // 2))

    @pl.when(me % 2 != 0)
    def _():
        for c in range(NC):
            copy_to(Y.at[0, y_parts[c]], Y.at[0, y_parts[c]], sx.at[0, c], rx.at[c], top).wait_recv()
    x_out[...] = (Y[0, :M, :] * srow).T
    ld_out[...] = Y[0, M:M + 1, 0:1]
    for l in range(height):
        @pl.when(gives[l])
        def _():
            copy_to(W, WB.at[l], sw.at[l], rw.at[l], me + 1 - (2 << l)).wait_send()
        @pl.when(left[l])
        def _():
            for c in range(NC):
                copy_to(Y.at[0, y_parts[c]], Y.at[0, y_parts[c]], sx.at[l, c], rx.at[c], me + (1 << l)).wait_send()
    @pl.when(rest)
    def _():
        for i, part in enumerate(s_parts):
            copy_to(Sx.at[part], SB.at[(0,) + part], sS.at[i], rS.at[0, i], top).wait_send()
        copy_to(GX, GB.at[0], sg, rg.at[0], top).wait_send()


def local(n, blocks, generators, rhs_blocks):
    R, M = rhs_blocks.shape
    height = n.bit_length() - 1
    dma = pltpu.SemaphoreType.DMA
    vm = lambda *s: pltpu.VMEM(s, F32)
    half = pltpu.VMEM((height + 1, R, R), B16)
    x, ld = pl.pallas_call(
        functools.partial(kernel, n),
        out_shape=(jax.ShapeDtypeStruct((R, M), F32), jax.ShapeDtypeStruct((1, 1), F32)),
        in_specs=[pl.BlockSpec(memory_space=pl.ANY)] * 3,
        out_specs=[pl.BlockSpec(memory_space=pltpu.VMEM)] * 2,
        scratch_shapes=[
            vm(R, R), vm(R, R), vm(R, M), vm(R, R), vm(R, R), vm(R, R), vm(height + 1, R, R), vm(height, R, R), vm(height, R + 8, M),
            vm(R + 8, M), vm(R, R + M), vm(R, R + M), vm(R, R), vm(R, R), vm(R, R), vm(R, R + M), vm(R, R + M), half, half,
            vm(height + 1, M, R), vm(height + 1, M + 8, R), vm(R // 2, 128), vm(8, 128), vm(G, 128),
            dma((3,)), dma((height,)), dma((height,)), dma((2,)), dma((height, 2)), dma, dma((height,)), dma((height, NC)), dma((NC,)),
        ],
        compiler_params=pltpu.CompilerParams(
            collective_id=0, has_side_effects=True, vmem_limit_bytes=48 * 1024 * 1024
        ),
        name="ulv",
    )(blocks, generators, rhs_blocks)
    return x, ld.reshape(())


def solution(mesh):
    n = mesh.shape["leaf"]
    return jax.shard_map(
        functools.partial(local, n),
        mesh=mesh,
        in_specs=(P("leaf", None), P("leaf", None), P("leaf", None)),
        out_specs=(P("leaf", None), P()),
        check_vma=False,
    )
```

```python
import functools

import jax
import jax.numpy as jnp
from jax import lax
from jax.experimental import pallas as pl
from jax.experimental.pallas import tpu as pltpu
from jax.sharding import PartitionSpec as P

F32 = jnp.float32
B16 = jnp.bfloat16
MESH = pl.DeviceIdType.MESH
G = 8
B = 64
NC = 2

def iota(shape, dim): return lax.broadcasted_iota(jnp.int32, shape, dim)

def group(tiles, pt, j, l, G, zero, put):
    b = tiles[0].shape[0]
    T = tiles[pt]
    call = [jnp.broadcast_to(T[j:, l+t:l+t+1], (b-j, 128)) for t in range(G)]
    c = [x[:G] + zero for x in call]
    D = [X[j:j+G] for X in tiles]
    lane = iota((8, 128), 1); sub = iota((G, 128), 0)
    for q in range(0, G, 4):
        p = lambda s, t: jnp.broadcast_to(c[q+t][q+s:q+s+1], (8, 128))
        a, bb, d = p(0,0), p(0,1), p(1,1)
        e, f, g, h = p(0,2), p(0,3), p(1,2), p(1,3)
        m, n, o = p(2,2), p(2,3), p(3,3)
        det1 = a*d - bb*bb
        i1 = 1.0/det1
        t00, t01 = d*e - bb*g, d*f - bb*h
        t10, t11 = a*g - bb*e, a*h - bb*f
        m2 = m - i1*(e*t00 + g*t10)
        n2 = n - i1*(e*t01 + g*t11)
        o2 = o - i1*(f*t01 + h*t11)
        det2 = m2*o2 - n2*n2
        i2 = 1.0/det2
        u00, u01, u10, u11 = i1*t00, i1*t01, i1*t10, i1*t11
        ia, ib, id_ = i1*a, i1*bb, i1*d
        ja, jb, jd = i2*m2, i2*n2, i2*o2
        put(None, j+q, (det1, det2))
        def solve(r):
            y0, y1 = id_*r[0] - ib*r[1], ia*r[1] - ib*r[0]
            z2 = r[2] - (e*y0 + g*y1)
            z3 = r[3] - (f*y0 + h*y1)
            w2 = jd*z2 - jb*z3
            w3 = ja*z3 - jb*z2
            w0 = (y0 - u01*w3) - u00*w2
            w1 = (y1 - u11*w3) - u10*w2
            return [w0, w1, w2, w3]
        def apply(X, piv):
            r = [jnp.broadcast_to(X[q+t:q+t+1], (8, 128)) for t in range(4)]
            if piv:
                inp = (lane >= l+q) & (lane < l+q+4)
                r = [jnp.where(inp, jnp.where(lane == l+q+t, 1.0, 0.0), r[t]) for t in range(4)]
            W = solve(r)
            w0, w1, w2, w3 = W
            out = []
            for v in range(G//8):
                xv = X[8*v:8*v+8]
                if piv: xv = jnp.where(inp, 0.0, xv)
                cv = [c[q+t][8*v:8*v+8] for t in range(4)]
                nv = (xv - (cv[2]*w2 + cv[3]*w3)) - (cv[0]*w0 + cv[1]*w1)
                if q//8 == v:
                    for t in range(4): nv = jnp.where(sub[:8] == q%8+t, W[t], nv)
                out.append(nv)
            return jnp.concatenate(out, 0) if len(out) > 1 else out[0]
        nc = list(c)
        if q + 4 < G:
            W = solve([c[q+t] for t in range(4)])
            for t in range(q+4, G):
                w = [jnp.broadcast_to(x[t:t+1], (8, 128)) for x in W]
                nv = (c[t] - (c[q+2]*w[2] + c[q+3]*w[3])) - (c[q]*w[0] + c[q+1]*w[1])
                for u in range(4): nv = jnp.where(sub[:8] == q+u, w[u], nv)
                nc[t] = nv
        D = [apply(D[i], i == pt) for i in range(len(tiles))]
        c = nc
    out = []
    inpG = (lane >= l) & (lane < l+G)
    for ti, X in enumerate(tiles):
        put(ti, j, D[ti])
        vs = [X[:j+G]]
        if j+G < b:
            R = [jnp.broadcast_to(D[ti][t:t+1], (8, 128)) for t in range(G)]
            for v in range(G//8, (b-j)//8):
                xv = X[j+8*v:j+8*v+8]
                if ti == pt: xv = jnp.where(inpG, 0.0, xv)
                acc = [None]*4
                for t in range(G):
                    pr = call[t][8*v:8*v+8]*R[t]
                    k = t % 4
                    acc[k] = pr if acc[k] is None else acc[k] + pr
                vs.append(xv - ((acc[0]+acc[1]) + (acc[2]+acc[3])))
        out.append(jnp.concatenate(vs, 0) if len(vs) > 1 else vs[0])
    return out

def split(x):
    hi = x.astype(B16); return hi, (x - hi.astype(F32)).astype(B16)
def mm3(a, b, dn):
    (ah, al), (bh, bl) = a, b
    dg = lambda u, v: lax.dot_general(u, v, dn, preferred_element_type=F32)
    return dg(ah, bh) + (dg(ah, bl) + dg(al, bh))
NN = (((1,), (0,)), ((), ()))
TN = (((0,), (0,)), ((), ()))
NT = (((1,), (1,)), ((), ()))


def copy_to(src, dst, send, recv, device):
    return pltpu.make_async_remote_copy(
        src_ref=src, dst_ref=dst, send_sem=send, recv_sem=recv, device_id=(device,), device_id_type=MESH
    )


def kernel(n, s_hbm, w_hbm, g_hbm, x_out, ld_out, s_in, w_in, g_in, S, Sx, W, WB, SB, GB, GX, Uo, CG, Rs, F, ZC, RC, E, Eh, El, DT, Y,
           det, ld_acc, zero_ref, sin, sw, rw, sS, rS, sg, rg, sx, sx2, rx):
    height = n.bit_length() - 1
    me = lax.axis_index("leaf")
    R, M = g_hbm.shape
    nk = R // B
    H = R // 2
    C = M // NC
    s_parts = [(slice(0, H), slice(0, R)), (slice(H, R), slice(H, R))]
    y_parts = [slice(C * c, C * c + C + (8 if c == NC - 1 else 0)) for c in range(NC)]
    left = [me % (2 << l) == 0 for l in range(height)]
    gives = [(me + 1) % (2 << l) == 0 for l in range(height)]
    rest = me != 0
    count = lambda flags: sum(f.astype(jnp.int32) for f in flags)
    span = 1 + sum(jnp.where(left[l], 1 << l, 0) for l in range(height))
    top = me - span
    upper = [(height - 1 - l) % 2 == 0 for l in range(height)]
    skips = [(l > 0) and upper[l] for l in range(height)]
    single = [left[l] if upper[l] else (me % (4 << l) == 0) for l in range(height)]
    double = [left[l] if skips[l] else (me % 2 > 1) for l in range(height)]
    far = sum(jnp.where((span == 1 << l) & (me // (2 << l) % 2 == 1), 2 << l, 0) for l in range(height) if not upper[l])
    source = top - far

    loads = [pltpu.make_async_copy(a, b, sin.at[i]) for i, (a, b) in enumerate([(s_hbm, s_in), (w_hbm, w_in), (g_hbm, g_in)])]
    for load in loads:
        load.start()
    barrier = pltpu.get_barrier_semaphore()
    for l in range(height):
        @pl.when(left[l])
        def _():
            pl.semaphore_signal(barrier, inc=1, device_id=(me + (2 << l) - 1,), device_id_type=MESH)
            pl.semaphore_signal(barrier, inc=1, device_id=(me + (1 << l),), device_id_type=MESH)
    @pl.when(rest)
    def _():
        pl.semaphore_signal(barrier, inc=1, device_id=(source,), device_id_type=MESH)

    loads[0].wait()
    s0 = s_in[...]
    eye = iota((R, R), 0) == iota((R, R), 1)
    diag = jnp.where(eye, s0, 0.0)
    drow = jnp.sum(diag, axis=0, keepdims=True)
    scol = lax.rsqrt(jnp.sum(diag, axis=1, keepdims=True))
    srow = lax.rsqrt(drow)
    S[...] = s0 * scol * srow
    loads[1].wait()
    W[...] = w_in[...] * scol
    loads[2].wait()
    CG[:, R:] = g_in[...] * scol
    zero_ref[...] = jnp.zeros_like(zero_ref)
    WB[height] = jnp.zeros((R, R), F32)
    ld_acc[...] = jnp.broadcast_to(jnp.sum(jnp.log(drow), axis=1, keepdims=True), (8, 128))
    pl.semaphore_wait(barrier, count(single) + count(double) + count(gives) + rest.astype(jnp.int32))

    def send_state(level, target):
        for i, part in enumerate(s_parts):
            Sx[part] = S[part]
            copy_to(Sx.at[part], SB.at[(level,) + part], sS.at[i], rS.at[level, i], target).start()

    def send_rhs(level, target):
        GX[:R, :] = CG[:, R:]
        GX[R:, :] = ld_acc[...]
        copy_to(GX, GB.at[level], sg, rg.at[level], target).start()

    @pl.when(me % 2 != 0)
    def _():
        send_state(0, me - 1)
    for l in range(height):
        @pl.when(gives[l])
        def _():
            copy_to(W, WB.at[l], sw.at[l], rw.at[l], me + 1 - (2 << l)).start()
    @pl.when(me % 2 != 0)
    def _():
        send_rhs(0, me - 1)

    row = iota((B, 128), 0)
    lane = iota((B, 128), 1)

    def level(it, st):
        last = it == height

        @pl.when(me % (2 * st) == 0)
        def _():
            @pl.when(jnp.logical_not(last))
            def _():
                copy_to(W, WB.at[it], sw.at[0], rw.at[it], me).wait_recv()
            zero = zero_ref[...]
            for k in range(nk):
                lb = (B * k) % 128
                base = B * k - lb
                lo = B * (k + 1)
                rows, pair = slice(B * k, lo), slice(base, base + 128)
                tiles = [S[rows, t:t + 128] for t in range(base, R, 128)]
                def put(ti, j, val):
                    if ti is None:
                        r0 = (rows.start + j) // 2
                        det[r0:r0 + 1, :] = val[0][0:1]
                        det[r0 + 1:r0 + 2, :] = val[1][0:1]
                    else:
                        Rs[rows.start + j:rows.start + j + G, base + 128 * ti:base + 128 * ti + 128] = val
                for j in range(0, B, G):
                    tiles = group(tiles, 0, j, lb + j, G, zero, put)
                Z = jnp.concatenate(tiles, 1) if len(tiles) > 1 else tiles[0]
                zs = split(Z)
                if k < nk - 1:
                    upd = mm3(zs, split(Rs[rows, base:]), TN)
                    S[lo:, base:] -= upd[lo - base:]
                if k == 0:
                    wb = WB[it]
                    CG[:, :R] = 0.5 * mm3(split(W[...]), split(wb), NT)
                rel = lane - lb
                inside = (rel >= 0) & (rel < B)
                Lk = jnp.where(inside & (rel < G * (row // G)), tiles[0], jnp.where(rel == row, 1.0, 0.0))
                DLk = jnp.where(inside & (rel < G * (row // G) + G), Rs[rows, pair], 0.0)
                both = mm3(split(jnp.concatenate([Lk, DLk], 0)), split(CG[pair, :]), NN)
                ZC[rows, :] = both[:B, :R]
                rc = both[B:]
                RC[rows, :] = rc
                ls = split(Lk)
                if k < nk - 1:
                    upd = mm3(zs, split(rc), TN)
                    CG[lo:, :] -= upd[lo - base:]
                    rs = Rs[rows, base:]
                    rs = jnp.where(iota(rs.shape, 1) >= lo - base, rs, 0.0)
                    ft = mm3(ls, split(rs), TN)[lb:lb + B]
                    F[rows, base:] = ft
                    ek = mm3(ls, split(rc), TN)[lb:lb + B]
                    E[rows, :] = ek
                    if k:
                        f = jnp.where((iota((B * k, 128), 1) >= lb) & (iota((B * k, 128), 1) < lb + B), F[:B * k, pair], 0.0)
                        gap = jnp.zeros_like
                        pad = (lambda v: jnp.concatenate([v, gap(v)], 0)) if lb == 0 else (lambda v: jnp.concatenate([gap(v), v], 0))
                        fs = split(f)
                        E[:B * k, :] -= mm3(fs, split(pad(ek)), NN)
                        F[:B * k, base:] -= mm3(fs, split(pad(ft)), NN)
                if k == nk - 2:
                    zc, rr = split(ZC[:lo, :]), split(RC[:lo, :])
                    Uo[:H, :] = mm3([a[:, :H] for a in zc], rr, TN)
                    Uo[H:, H:] = mm3([a[:, H:] for a in zc], [a[:, H:] for a in rr], TN)

            ek = mm3(ls, split(rc), TN)[lb:]
            E[rows, :] = ek
            f = jnp.where(iota((R - B, 128), 1) >= lb, F[:R - B, pair], 0.0)
            E[:R - B, :] -= mm3(split(f), split(jnp.concatenate([jnp.zeros_like(ek), ek], 0)), NN)
            et = E[...]
            Eh[it], El[it] = split(et[:, :R].T)
            DT[it] = et[:, R:].T
            ld_acc[...] += jnp.broadcast_to(jnp.sum(jnp.log(det[...]), axis=0, keepdims=True), (8, 128))

            @pl.when(jnp.logical_not(last))
            def _():
                for i, part in enumerate(s_parts):
                    copy_to(Sx.at[part], SB.at[(it,) + part], sS.at[i], rS.at[it, i], me).wait_recv()
                zc, rr = split(ZC[rows, :]), split(RC[rows, :])
                ua = Uo[:H, :] + mm3([a[:, :H] for a in zc], rr, TN)
                ub = Uo[H:, H:] + mm3([a[:, H:] for a in zc], [a[:, H:] for a in rr], TN)
                S[:H, :] = SB[it, :H, :] - ua[:, :R]
                S[H:, H:] = SB[it, H:, H:] - ub[:, :H]
                turn = me % (4 * st) != 0
                @pl.when(turn)
                def _():
                    send_state(it + 1, top)
                copy_to(GX, GB.at[it], sg, rg.at[it], me).wait_recv()
                CG[:H, R:] = GB[it, :H] - ua[:, R:]
                CG[H:, R:] = GB[it, H:R] - ub[:, H:]
                ld_acc[...] += GB[it, R:]
                @pl.when(turn)
                def _():
                    send_rhs(it + 1, top)
                W[...] = WB[it]
        return st * 2

    lax.fori_loop(0, height + 1, level, jnp.int32(1))

    @pl.when(jnp.logical_not(rest))
    def _():
        Y[height, :M, :] = DT[height]
        Y[height, M:, :] = jnp.broadcast_to(ld_acc[0:1, 0:1] / (R * n), (8, R))

    def down(i, st):
        it = height - 1 - i

        @pl.when(me % (2 * st) == 0)
        def _():
            high = i % 2 == 0
            for c in range(NC):
                part = Y.at[it + 1, y_parts[c]]
                @pl.when(rest & (span == 2 * st))
                def _():
                    copy_to(part, part, sx.at[it, c], rx.at[c], me).wait_recv()
                @pl.when(high | (me % (4 * st) == 0))
                def _():
                    copy_to(part, Y.at[it, y_parts[c]], sx.at[it, c], rx.at[c], me + st).start()
                @pl.when(high & (it > 0))
                def _():
                    copy_to(part, Y.at[it - 1, y_parts[c]], sx2.at[it, c], rx.at[c], me + st + st // 2).start()
            for c in range(NC):
                r = slice(C * c, C * c + C)
                ah, al = split(Y[it + 1, r, :])
                dg = lambda a, b: jnp.dot(a, b, preferred_element_type=F32)
                Y[it, r, :] = DT[it, r, :] - (dg(ah, Eh[it]) + (dg(al, Eh[it]) + dg(ah, El[it])))
            Y[it, M:, :] = Y[it + 1, M:, :]
        return st // 2

    lax.fori_loop(0, height, down, jnp.int32(n // 2))

    @pl.when(me % 2 != 0)
    def _():
        for c in range(NC):
            copy_to(Y.at[0, y_parts[c]], Y.at[0, y_parts[c]], sx.at[0, c], rx.at[c], source).wait_recv()
    x_out[...] = (Y[0, :M, :] * srow).T
    ld_out[...] = Y[0, M:M + 1, 0:1]
    for l in range(height):
        @pl.when(gives[l])
        def _():
            copy_to(W, WB.at[l], sw.at[l], rw.at[l], me + 1 - (2 << l)).wait_send()
        @pl.when(single[l])
        def _():
            for c in range(NC):
                copy_to(Y.at[0, y_parts[c]], Y.at[0, y_parts[c]], sx.at[l, c], rx.at[c], me + (1 << l)).wait_send()
        @pl.when(double[l])
        def _():
            for c in range(NC):
                copy_to(Y.at[0, y_parts[c]], Y.at[0, y_parts[c]], sx2.at[l, c], rx.at[c], me + (1 << l)).wait_send()
    @pl.when(rest)
    def _():
        for i, part in enumerate(s_parts):
            copy_to(Sx.at[part], SB.at[(0,) + part], sS.at[i], rS.at[0, i], top).wait_send()
        copy_to(GX, GB.at[0], sg, rg.at[0], top).wait_send()


def local(n, blocks, generators, rhs_blocks):
    R, M = rhs_blocks.shape
    height = n.bit_length() - 1
    dma = pltpu.SemaphoreType.DMA
    vm = lambda *s: pltpu.VMEM(s, F32)
    half = pltpu.VMEM((height + 1, R, R), B16)
    x, ld = pl.pallas_call(
        functools.partial(kernel, n),
        out_shape=(jax.ShapeDtypeStruct((R, M), F32), jax.ShapeDtypeStruct((1, 1), F32)),
        in_specs=[pl.BlockSpec(memory_space=pl.ANY)] * 3,
        out_specs=[pl.BlockSpec(memory_space=pltpu.VMEM)] * 2,
        scratch_shapes=[
            vm(R, R), vm(R, R), vm(R, M), vm(R, R), vm(R, R), vm(R, R), vm(height + 1, R, R), vm(height, R, R), vm(height, R + 8, M),
            vm(R + 8, M), vm(R, R + M), vm(R, R + M), vm(R, R), vm(R, R), vm(R, R), vm(R, R + M), vm(R, R + M), half, half,
            vm(height + 1, M, R), vm(height + 1, M + 8, R), vm(R // 2, 128), vm(8, 128), vm(G, 128),
            dma((3,)), dma((height,)), dma((height,)), dma((2,)), dma((height, 2)), dma, dma((height,)), dma((height, NC)), dma((height, NC)), dma((NC,)),
        ],
        compiler_params=pltpu.CompilerParams(
            collective_id=0, has_side_effects=True, vmem_limit_bytes=60 * 1024 * 1024
        ),
        name="ulv",
    )(blocks, generators, rhs_blocks)
    return x, ld.reshape(())


def solution(mesh):
    n = mesh.shape["leaf"]
    return jax.shard_map(
        functools.partial(local, n),
        mesh=mesh,
        in_specs=(P("leaf", None), P("leaf", None), P("leaf", None)),
        out_specs=(P("leaf", None), P()),
        check_vma=False,
    )
```

```python
import functools

import jax
import jax.numpy as jnp
from jax import lax
from jax.experimental import pallas as pl
from jax.experimental.pallas import tpu as pltpu
from jax.sharding import PartitionSpec as P

F32 = jnp.float32
B16 = jnp.bfloat16
MESH = pl.DeviceIdType.MESH
G = 8
B = 64
NC = 2

def iota(shape, dim): return lax.broadcasted_iota(jnp.int32, shape, dim)

def sweep(tiles, pt, l, G, zero, put):
    b = tiles[0].shape[0]
    spread = lambda r, c0: [jnp.broadcast_to(tiles[pt][r:r + G, c0+t:c0+t+1], (G, 128)) for t in range(G)]
    c = None
    for j in range(0, b, G):
        if c is None:
            c = [x + zero for x in spread(j, l + j)]
        ahead = later = None
        if j + G < b:
            ahead, later = spread(j + G, l + j), spread(j + G, l + j + G)
        tiles, c = half(tiles, pt, j, l + j, G, c, ahead, later, zero, put)
    return tiles


def half(tiles, pt, j, l, G, c, ahead, later, zero, put):
    b = tiles[0].shape[0]
    T = tiles[pt]
    D = [X[j:j+G] for X in tiles]
    low = [jnp.broadcast_to(T[j+G:, l+t:l+t+1], (b-j-G, 128)) for t in range(G)] if j+G < b else None
    lane = iota((8, 128), 1); sub = iota((G, 128), 0)
    if ahead is not None:
        A = [x + zero for x in ahead]
        V = list(A)
    for q in range(0, G, 4):
        p = lambda s, t: jnp.broadcast_to(c[q+t][q+s:q+s+1], (8, 128))
        a, bb, d = p(0,0), p(0,1), p(1,1)
        e, f, g, h = p(0,2), p(0,3), p(1,2), p(1,3)
        m, n, o = p(2,2), p(2,3), p(3,3)
        det1 = a*d - bb*bb
        i1 = 1.0/det1
        t00, t01 = d*e - bb*g, d*f - bb*h
        t10, t11 = a*g - bb*e, a*h - bb*f
        m2 = m - i1*(e*t00 + g*t10)
        n2 = n - i1*(e*t01 + g*t11)
        o2 = o - i1*(f*t01 + h*t11)
        det2 = m2*o2 - n2*n2
        i2 = 1.0/det2
        u00, u01, u10, u11 = i1*t00, i1*t01, i1*t10, i1*t11
        ia, ib, id_ = i1*a, i1*bb, i1*d
        ja, jb, jd = i2*m2, i2*n2, i2*o2
        put(None, j+q, (det1, det2))
        cs = lambda u, t, c=c: jnp.broadcast_to(c[t][u:u+1], (8, 128))
        def solve(r):
            y0, y1 = id_*r[0] - ib*r[1], ia*r[1] - ib*r[0]
            z2 = r[2] - (e*y0 + g*y1)
            z3 = r[3] - (f*y0 + h*y1)
            w2 = jd*z2 - jb*z3
            w3 = ja*z3 - jb*z2
            w0 = (y0 - u01*w3) - u00*w2
            w1 = (y1 - u11*w3) - u10*w2
            return [w0, w1, w2, w3]
        def apply(X, piv):
            r = [jnp.broadcast_to(X[q+t:q+t+1], (8, 128)) for t in range(4)]
            if piv:
                inp = (lane >= l+q) & (lane < l+q+4)
                r = [jnp.where(inp, jnp.where(lane == l+q+t, 1.0, 0.0), r[t]) for t in range(4)]
            W = solve(r)
            w0, w1, w2, w3 = W
            out = []
            for v in range(G//8):
                xv = X[8*v:8*v+8]
                if piv: xv = jnp.where(inp, 0.0, xv)
                cv = [c[q+t][8*v:8*v+8] for t in range(4)]
                nv = (xv - (cv[2]*w2 + cv[3]*w3)) - (cv[0]*w0 + cv[1]*w1)
                if q//8 == v:
                    for t in range(4): nv = jnp.where(sub[:8] == q%8+t, W[t], nv)
                out.append(nv)
            return jnp.concatenate(out, 0) if len(out) > 1 else out[0]
        nc = list(c)
        if q + 4 < G:
            W = solve([c[q+t] for t in range(4)])
            for t in range(q+4, G):
                w = [jnp.broadcast_to(x[t:t+1], (8, 128)) for x in W]
                nv = (c[t] - (c[q+2]*w[2] + c[q+3]*w[3])) - (c[q]*w[0] + c[q+1]*w[1])
                for u in range(4): nv = jnp.where(sub[:8] == q+u, w[u], nv)
                nc[t] = nv
        if ahead is not None:
            W = solve(V[q:q+4])
            for u in range(G):
                if not q <= u < q + 4:
                    V[u] = (V[u] - (cs(u, q+2)*W[2] + cs(u, q+3)*W[3])) - (cs(u, q)*W[0] + cs(u, q+1)*W[1])
            V[q:q+4] = W
        D = [apply(D[i], i == pt) for i in range(len(tiles))]
        c = nc
    out = []
    if ahead is not None:
        fresh = []
        for t in range(G):
            acc = [None]*4
            for u in range(G):
                pr = A[u]*jnp.broadcast_to(V[u][t:t+1], (8, 128))
                acc[u % 4] = pr if acc[u % 4] is None else acc[u % 4] + pr
            fresh.append((later[t] + zero) - ((acc[0]+acc[1]) + (acc[2]+acc[3])))
        later = fresh
    inpG = (lane >= l) & (lane < l+G)
    for ti, X in enumerate(tiles):
        put(ti, j, D[ti])
        vs = [X[:j+G]]
        if j+G < b:
            R = [jnp.broadcast_to(D[ti][t:t+1], (8, 128)) for t in range(G)]
            for v in range(G//8, (b-j)//8):
                xv = X[j+8*v:j+8*v+8]
                if ti == pt: xv = jnp.where(inpG, 0.0, xv)
                acc = [None]*4
                for t in range(G):
                    pr = low[t][8*(v-G//8):8*(v-G//8)+8]*R[t]
                    k = t % 4
                    acc[k] = pr if acc[k] is None else acc[k] + pr
                vs.append(xv - ((acc[0]+acc[1]) + (acc[2]+acc[3])))
        out.append(jnp.concatenate(vs, 0) if len(vs) > 1 else vs[0])
    return out, later

def split(x):
    hi = x.astype(B16); return hi, (x - hi.astype(F32)).astype(B16)
def mm3(a, b, dn):
    (ah, al), (bh, bl) = a, b
    dg = lambda u, v: lax.dot_general(u, v, dn, preferred_element_type=F32)
    return dg(ah, bh) + (dg(ah, bl) + dg(al, bh))
NN = (((1,), (0,)), ((), ()))
TN = (((0,), (0,)), ((), ()))
NT = (((1,), (1,)), ((), ()))


def copy_to(src, dst, send, recv, device):
    return pltpu.make_async_remote_copy(
        src_ref=src, dst_ref=dst, send_sem=send, recv_sem=recv, device_id=(device,), device_id_type=MESH
    )


def kernel(n, s_hbm, w_hbm, g_hbm, x_out, ld_out, s_in, w_in, g_in, S, Sx, W, WB, SB, GB, GX, Uo, CG, Rs, F, ZC, RC, E, Eh, El, DT, Y,
           det, ld_acc, zero_ref, sin, sw, rw, sS, rS, sg, rg, sx, sx2, rx):
    height = n.bit_length() - 1
    me = lax.axis_index("leaf")
    R, M = g_hbm.shape
    nk = R // B
    H = R // 2
    C = M // NC
    s_parts = [(slice(0, H), slice(0, R)), (slice(H, R), slice(H, R))]
    y_parts = [slice(C * c, C * c + C + (8 if c == NC - 1 else 0)) for c in range(NC)]
    left = [me % (2 << l) == 0 for l in range(height)]
    gives = [(me + 1) % (2 << l) == 0 for l in range(height)]
    rest = me != 0
    count = lambda flags: sum(f.astype(jnp.int32) for f in flags)
    span = 1 + sum(jnp.where(left[l], 1 << l, 0) for l in range(height))
    top = me - span
    upper = [(height - 1 - l) % 2 == 0 for l in range(height)]
    skips = [(l > 0) and upper[l] for l in range(height)]
    single = [left[l] if upper[l] else (me % (4 << l) == 0) for l in range(height)]
    double = [left[l] if skips[l] else (me % 2 > 1) for l in range(height)]
    far = sum(jnp.where((span == 1 << l) & (me // (2 << l) % 2 == 1), 2 << l, 0) for l in range(height) if not upper[l])
    source = top - far

    loads = [pltpu.make_async_copy(a, b, sin.at[i]) for i, (a, b) in enumerate([(s_hbm, s_in), (w_hbm, w_in), (g_hbm, g_in)])]
    for load in loads:
        load.start()
    barrier = pltpu.get_barrier_semaphore()
    for l in range(height):
        @pl.when(left[l])
        def _():
            pl.semaphore_signal(barrier, inc=1, device_id=(me + (2 << l) - 1,), device_id_type=MESH)
            pl.semaphore_signal(barrier, inc=1, device_id=(me + (1 << l),), device_id_type=MESH)
    @pl.when(rest)
    def _():
        pl.semaphore_signal(barrier, inc=1, device_id=(source,), device_id_type=MESH)

    loads[0].wait()
    s0 = s_in[...]
    eye = iota((R, R), 0) == iota((R, R), 1)
    diag = jnp.where(eye, s0, 0.0)
    drow = jnp.sum(diag, axis=0, keepdims=True)
    scol = lax.rsqrt(jnp.sum(diag, axis=1, keepdims=True))
    srow = lax.rsqrt(drow)
    S[...] = s0 * scol * srow
    loads[1].wait()
    W[...] = w_in[...] * scol
    loads[2].wait()
    CG[:, R:] = g_in[...] * scol
    zero_ref[...] = jnp.zeros_like(zero_ref)
    WB[height] = jnp.zeros((R, R), F32)
    ld_acc[...] = jnp.broadcast_to(jnp.sum(jnp.log(drow), axis=1, keepdims=True), (8, 128))
    pl.semaphore_wait(barrier, count(single) + count(double) + count(gives) + rest.astype(jnp.int32))

    def send_state(level, target):
        for i, part in enumerate(s_parts):
            Sx[part] = S[part]
            copy_to(Sx.at[part], SB.at[(level,) + part], sS.at[i], rS.at[level, i], target).start()

    def send_rhs(level, target):
        GX[:R, :] = CG[:, R:]
        GX[R:, :] = ld_acc[...]
        copy_to(GX, GB.at[level], sg, rg.at[level], target).start()

    @pl.when(me % 2 != 0)
    def _():
        send_state(0, me - 1)
    for l in range(height):
        @pl.when(gives[l])
        def _():
            copy_to(W, WB.at[l], sw.at[l], rw.at[l], me + 1 - (2 << l)).start()
    @pl.when(me % 2 != 0)
    def _():
        send_rhs(0, me - 1)

    row = iota((B, 128), 0)
    lane = iota((B, 128), 1)

    def level(it, st):
        last = it == height

        @pl.when(me % (2 * st) == 0)
        def _():
            @pl.when(jnp.logical_not(last))
            def _():
                copy_to(W, WB.at[it], sw.at[0], rw.at[it], me).wait_recv()
            for k in range(nk):
                lb = (B * k) % 128
                base = B * k - lb
                lo = B * (k + 1)
                rows, pair = slice(B * k, lo), slice(base, base + 128)
                def eliminate():
                    tiles = [S[rows, t:t + 128] for t in range(base, R, 128)]
                    def put(ti, j, val):
                        if ti is None:
                            r0 = (rows.start + j) // 2
                            det[r0:r0 + 1, :] = val[0][0:1]
                            det[r0 + 1:r0 + 2, :] = val[1][0:1]
                        else:
                            Rs[rows.start + j:rows.start + j + G, base + 128 * ti:base + 128 * ti + 128] = val
                    tiles = sweep(tiles, 0, lb, G, zero_ref[...], put)
                    for i, t in enumerate(tiles):
                        S[rows, base + 128 * i:base + 128 * i + 128] = t
                eliminate()
                Z = S[rows, base:]
                zs = split(Z)
                if k < nk - 1:
                    upd = mm3(zs, split(Rs[rows, base:]), TN)
                    S[lo:, base:] -= upd[lo - base:]
                if k == 0:
                    wb = WB[it]
                    CG[:, :R] = 0.5 * mm3(split(W[...]), split(wb), NT)
                rel = lane - lb
                inside = (rel >= 0) & (rel < B)
                Lk = jnp.where(inside & (rel < G * (row // G)), Z[:, :128], jnp.where(rel == row, 1.0, 0.0))
                DLk = jnp.where(inside & (rel < G * (row // G) + G), Rs[rows, pair], 0.0)
                both = mm3(split(jnp.concatenate([Lk, DLk], 0)), split(CG[pair, :]), NN)
                ZC[rows, :] = both[:B, :R]
                rc = both[B:]
                RC[rows, :] = rc
                ls = split(Lk)
                if k < nk - 1:
                    upd = mm3(zs, split(rc), TN)
                    CG[lo:, :] -= upd[lo - base:]
                    rs = Rs[rows, base:]
                    rs = jnp.where(iota(rs.shape, 1) >= lo - base, rs, 0.0)
                    ft = mm3(ls, split(rs), TN)[lb:lb + B]
                    F[rows, base:] = ft
                    ek = mm3(ls, split(rc), TN)[lb:lb + B]
                    E[rows, :] = ek
                    if k:
                        f = jnp.where((iota((B * k, 128), 1) >= lb) & (iota((B * k, 128), 1) < lb + B), F[:B * k, pair], 0.0)
                        gap = jnp.zeros_like
                        pad = (lambda v: jnp.concatenate([v, gap(v)], 0)) if lb == 0 else (lambda v: jnp.concatenate([gap(v), v], 0))
                        fs = split(f)
                        E[:B * k, :] -= mm3(fs, split(pad(ek)), NN)
                        F[:B * k, base:] -= mm3(fs, split(pad(ft)), NN)
                if k == nk - 2:
                    zc, rr = split(ZC[:lo, :]), split(RC[:lo, :])
                    Uo[:H, :] = mm3([a[:, :H] for a in zc], rr, TN)
                    Uo[H:, H:] = mm3([a[:, H:] for a in zc], [a[:, H:] for a in rr], TN)

            ek = mm3(ls, split(rc), TN)[lb:]
            E[rows, :] = ek
            f = jnp.where(iota((R - B, 128), 1) >= lb, F[:R - B, pair], 0.0)
            E[:R - B, :] -= mm3(split(f), split(jnp.concatenate([jnp.zeros_like(ek), ek], 0)), NN)
            et = E[...]
            Eh[it], El[it] = split(et[:, :R].T)
            DT[it] = et[:, R:].T
            ld_acc[...] += jnp.broadcast_to(jnp.sum(jnp.log(det[...]), axis=0, keepdims=True), (8, 128))

            @pl.when(jnp.logical_not(last))
            def _():
                for i, part in enumerate(s_parts):
                    copy_to(Sx.at[part], SB.at[(it,) + part], sS.at[i], rS.at[it, i], me).wait_recv()
                zc, rr = split(ZC[rows, :]), split(RC[rows, :])
                ua = Uo[:H, :] + mm3([a[:, :H] for a in zc], rr, TN)
                ub = Uo[H:, H:] + mm3([a[:, H:] for a in zc], [a[:, H:] for a in rr], TN)
                S[:H, :] = SB[it, :H, :] - ua[:, :R]
                S[H:, H:] = SB[it, H:, H:] - ub[:, :H]
                turn = me % (4 * st) != 0
                @pl.when(turn)
                def _():
                    send_state(it + 1, top)
                copy_to(GX, GB.at[it], sg, rg.at[it], me).wait_recv()
                CG[:H, R:] = GB[it, :H] - ua[:, R:]
                CG[H:, R:] = GB[it, H:R] - ub[:, H:]
                ld_acc[...] += GB[it, R:]
                @pl.when(turn)
                def _():
                    send_rhs(it + 1, top)
                W[...] = WB[it]
        return st * 2

    lax.fori_loop(0, height + 1, level, jnp.int32(1))

    @pl.when(jnp.logical_not(rest))
    def _():
        Y[height, :M, :] = DT[height]
        Y[height, M:, :] = jnp.broadcast_to(ld_acc[0:1, 0:1] / (R * n), (8, R))

    def down(i, st):
        it = height - 1 - i

        @pl.when(me % (2 * st) == 0)
        def _():
            high = i % 2 == 0
            for c in range(NC):
                part = Y.at[it + 1, y_parts[c]]
                @pl.when(rest & (span == 2 * st))
                def _():
                    copy_to(part, part, sx.at[it, c], rx.at[c], me).wait_recv()
                @pl.when(high | (me % (4 * st) == 0))
                def _():
                    copy_to(part, Y.at[it, y_parts[c]], sx.at[it, c], rx.at[c], me + st).start()
                @pl.when(high & (it > 0))
                def _():
                    copy_to(part, Y.at[it - 1, y_parts[c]], sx2.at[it, c], rx.at[c], me + st + st // 2).start()
            for c in range(NC):
                r = slice(C * c, C * c + C)
                ah, al = split(Y[it + 1, r, :])
                dg = lambda a, b: jnp.dot(a, b, preferred_element_type=F32)
                Y[it, r, :] = DT[it, r, :] - (dg(ah, Eh[it]) + (dg(al, Eh[it]) + dg(ah, El[it])))
            Y[it, M:, :] = Y[it + 1, M:, :]
        return st // 2

    lax.fori_loop(0, height, down, jnp.int32(n // 2))

    @pl.when(me % 2 != 0)
    def _():
        for c in range(NC):
            copy_to(Y.at[0, y_parts[c]], Y.at[0, y_parts[c]], sx.at[0, c], rx.at[c], source).wait_recv()
    x_out[...] = (Y[0, :M, :] * srow).T
    ld_out[...] = Y[0, M:M + 1, 0:1]
    for l in range(height):
        @pl.when(gives[l])
        def _():
            copy_to(W, WB.at[l], sw.at[l], rw.at[l], me + 1 - (2 << l)).wait_send()
        @pl.when(single[l])
        def _():
            for c in range(NC):
                copy_to(Y.at[0, y_parts[c]], Y.at[0, y_parts[c]], sx.at[l, c], rx.at[c], me + (1 << l)).wait_send()
        @pl.when(double[l])
        def _():
            for c in range(NC):
                copy_to(Y.at[0, y_parts[c]], Y.at[0, y_parts[c]], sx2.at[l, c], rx.at[c], me + (1 << l)).wait_send()
    @pl.when(rest)
    def _():
        for i, part in enumerate(s_parts):
            copy_to(Sx.at[part], SB.at[(0,) + part], sS.at[i], rS.at[0, i], top).wait_send()
        copy_to(GX, GB.at[0], sg, rg.at[0], top).wait_send()


def local(n, blocks, generators, rhs_blocks):
    R, M = rhs_blocks.shape
    height = n.bit_length() - 1
    dma = pltpu.SemaphoreType.DMA
    vm = lambda *s: pltpu.VMEM(s, F32)
    half = pltpu.VMEM((height + 1, R, R), B16)
    x, ld = pl.pallas_call(
        functools.partial(kernel, n),
        out_shape=(jax.ShapeDtypeStruct((R, M), F32), jax.ShapeDtypeStruct((1, 1), F32)),
        in_specs=[pl.BlockSpec(memory_space=pl.ANY)] * 3,
        out_specs=[pl.BlockSpec(memory_space=pltpu.VMEM)] * 2,
        scratch_shapes=[
            vm(R, R), vm(R, R), vm(R, M), vm(R, R), vm(R, R), vm(R, R), vm(height + 1, R, R), vm(height, R, R), vm(height, R + 8, M),
            vm(R + 8, M), vm(R, R + M), vm(R, R + M), vm(R, R), vm(R, R), vm(R, R), vm(R, R + M), vm(R, R + M), half, half,
            vm(height + 1, M, R), vm(height + 1, M + 8, R), vm(R // 2, 128), vm(8, 128), vm(G, 128),
            dma((3,)), dma((height,)), dma((height,)), dma((2,)), dma((height, 2)), dma, dma((height,)), dma((height, NC)), dma((height, NC)), dma((NC,)),
        ],
        compiler_params=pltpu.CompilerParams(
            collective_id=0, has_side_effects=True, vmem_limit_bytes=60 * 1024 * 1024
        ),
        name="ulv",
    )(blocks, generators, rhs_blocks)
    return x, ld.reshape(())


def solution(mesh):
    n = mesh.shape["leaf"]
    return jax.shard_map(
        functools.partial(local, n),
        mesh=mesh,
        in_specs=(P("leaf", None), P("leaf", None), P("leaf", None)),
        out_specs=(P("leaf", None), P()),
        check_vma=False,
    )
```

```python
import functools

import jax
import jax.numpy as jnp
from jax import lax
from jax.experimental import pallas as pl
from jax.experimental.pallas import tpu as pltpu
from jax.sharding import PartitionSpec as P

F32 = jnp.float32
B16 = jnp.bfloat16
MESH = pl.DeviceIdType.MESH
G = 8
B = 64
NC = 2

def iota(shape, dim): return lax.broadcasted_iota(jnp.int32, shape, dim)

def sweep(tiles, pt, l, G, zero, put):
    b = tiles[0].shape[0]
    spread = lambda r, c0: [jnp.broadcast_to(tiles[pt][r:r + G, c0+t:c0+t+1], (G, 128)) for t in range(G)]
    c = None
    for j in range(0, b, G):
        if c is None:
            c = [x + zero for x in spread(j, l + j)]
        ahead = later = None
        if j + G < b:
            ahead, later = spread(j + G, l + j), spread(j + G, l + j + G)
        tiles, c = half(tiles, pt, j, l + j, G, c, ahead, later, zero, put)
    return tiles


def half(tiles, pt, j, l, G, c, ahead, later, zero, put):
    b = tiles[0].shape[0]
    T = tiles[pt]
    D = [X[j:j+G] for X in tiles]
    low = [jnp.broadcast_to(T[j+G:, l+t:l+t+1], (b-j-G, 128)) for t in range(G)] if j+G < b else None
    lane = iota((8, 128), 1); sub = iota((G, 128), 0)
    if ahead is not None:
        A = [x + zero for x in ahead]
        V = list(A)
    for q in range(0, G, 4):
        p = lambda s, t: jnp.broadcast_to(c[q+t][q+s:q+s+1], (8, 128))
        a, bb, d = p(0,0), p(0,1), p(1,1)
        e, f, g, h = p(0,2), p(0,3), p(1,2), p(1,3)
        m, n, o = p(2,2), p(2,3), p(3,3)
        det1 = a*d - bb*bb
        i1 = 1.0/det1
        t00, t01 = d*e - bb*g, d*f - bb*h
        t10, t11 = a*g - bb*e, a*h - bb*f
        m2 = m - i1*(e*t00 + g*t10)
        n2 = n - i1*(e*t01 + g*t11)
        o2 = o - i1*(f*t01 + h*t11)
        det2 = m2*o2 - n2*n2
        i2 = 1.0/det2
        u00, u01, u10, u11 = i1*t00, i1*t01, i1*t10, i1*t11
        ia, ib, id_ = i1*a, i1*bb, i1*d
        ja, jb, jd = i2*m2, i2*n2, i2*o2
        put(None, j+q, (det1, det2))
        cs = lambda u, t, c=c: jnp.broadcast_to(c[t][u:u+1], (8, 128))
        def solve(r):
            y0, y1 = id_*r[0] - ib*r[1], ia*r[1] - ib*r[0]
            z2 = r[2] - (e*y0 + g*y1)
            z3 = r[3] - (f*y0 + h*y1)
            w2 = jd*z2 - jb*z3
            w3 = ja*z3 - jb*z2
            w0 = (y0 - u01*w3) - u00*w2
            w1 = (y1 - u11*w3) - u10*w2
            return [w0, w1, w2, w3]
        def apply(X, piv):
            r = [jnp.broadcast_to(X[q+t:q+t+1], (8, 128)) for t in range(4)]
            if piv:
                inp = (lane >= l+q) & (lane < l+q+4)
                r = [jnp.where(inp, jnp.where(lane == l+q+t, 1.0, 0.0), r[t]) for t in range(4)]
            W = solve(r)
            w0, w1, w2, w3 = W
            out = []
            for v in range(G//8):
                xv = X[8*v:8*v+8]
                if piv: xv = jnp.where(inp, 0.0, xv)
                cv = [c[q+t][8*v:8*v+8] for t in range(4)]
                nv = (xv - (cv[2]*w2 + cv[3]*w3)) - (cv[0]*w0 + cv[1]*w1)
                if q//8 == v:
                    for t in range(4): nv = jnp.where(sub[:8] == q%8+t, W[t], nv)
                out.append(nv)
            return jnp.concatenate(out, 0) if len(out) > 1 else out[0]
        nc = list(c)
        if q + 4 < G:
            W = solve([c[q+t] for t in range(4)])
            for t in range(q+4, G):
                w = [jnp.broadcast_to(x[t:t+1], (8, 128)) for x in W]
                nv = (c[t] - (c[q+2]*w[2] + c[q+3]*w[3])) - (c[q]*w[0] + c[q+1]*w[1])
                for u in range(4): nv = jnp.where(sub[:8] == q+u, w[u], nv)
                nc[t] = nv
        if ahead is not None:
            W = solve(V[q:q+4])
            for u in range(G):
                if not q <= u < q + 4:
                    V[u] = (V[u] - (cs(u, q+2)*W[2] + cs(u, q+3)*W[3])) - (cs(u, q)*W[0] + cs(u, q+1)*W[1])
            V[q:q+4] = W
        D = [apply(D[i], i == pt) for i in range(len(tiles))]
        c = nc
    out = []
    if ahead is not None:
        fresh = []
        for t in range(G):
            acc = [None]*4
            for u in range(G):
                pr = A[u]*jnp.broadcast_to(V[u][t:t+1], (8, 128))
                acc[u % 4] = pr if acc[u % 4] is None else acc[u % 4] + pr
            fresh.append((later[t] + zero) - ((acc[0]+acc[1]) + (acc[2]+acc[3])))
        later = fresh
    inpG = (lane >= l) & (lane < l+G)
    for ti, X in enumerate(tiles):
        put(ti, j, D[ti])
        vs = [X[:j+G]]
        if j+G < b:
            R = [jnp.broadcast_to(D[ti][t:t+1], (8, 128)) for t in range(G)]
            for v in range(G//8, (b-j)//8):
                xv = X[j+8*v:j+8*v+8]
                if ti == pt: xv = jnp.where(inpG, 0.0, xv)
                acc = [None]*4
                for t in range(G):
                    pr = low[t][8*(v-G//8):8*(v-G//8)+8]*R[t]
                    k = t % 4
                    acc[k] = pr if acc[k] is None else acc[k] + pr
                vs.append(xv - ((acc[0]+acc[1]) + (acc[2]+acc[3])))
        out.append(jnp.concatenate(vs, 0) if len(vs) > 1 else vs[0])
    return out, later

def split(x):
    hi = x.astype(B16); return hi, (x - hi.astype(F32)).astype(B16)
def mm3(a, b, dn):
    (ah, al), (bh, bl) = a, b
    dg = lambda u, v: lax.dot_general(u, v, dn, preferred_element_type=F32)
    return dg(ah, bh) + (dg(ah, bl) + dg(al, bh))
NN = (((1,), (0,)), ((), ()))
TN = (((0,), (0,)), ((), ()))
NT = (((1,), (1,)), ((), ()))


def copy_to(src, dst, send, recv, device):
    return pltpu.make_async_remote_copy(
        src_ref=src, dst_ref=dst, send_sem=send, recv_sem=recv, device_id=(device,), device_id_type=MESH
    )


def kernel(n, s_hbm, w_hbm, g_hbm, x_out, ld_out, s_in, w_in, g_in, S, Sx, W, WB, SB, GB, GX, Uo, CG, Rs, F, ZC, RC, L3, E, Eh, El, DT, Y,
           det, ld_acc, zero_ref, sin, sw, rw, sS, rS, sg, rg, sx, sx2, rx):
    height = n.bit_length() - 1
    me = lax.axis_index("leaf")
    R, M = g_hbm.shape
    nk = R // B
    H = R // 2
    C = M // NC
    s_parts = [(slice(0, H), slice(0, R)), (slice(H, R), slice(H, R))]
    y_parts = [slice(C * c, C * c + C + (8 if c == NC - 1 else 0)) for c in range(NC)]
    left = [me % (2 << l) == 0 for l in range(height)]
    gives = [(me + 1) % (2 << l) == 0 for l in range(height)]
    rest = me != 0
    count = lambda flags: sum(f.astype(jnp.int32) for f in flags)
    span = 1 + sum(jnp.where(left[l], 1 << l, 0) for l in range(height))
    top = me - span
    upper = [(height - 1 - l) % 2 == 0 for l in range(height)]
    skips = [(l > 0) and upper[l] for l in range(height)]
    single = [left[l] if upper[l] else (me % (4 << l) == 0) for l in range(height)]
    double = [left[l] if skips[l] else (me % 2 > 1) for l in range(height)]
    far = sum(jnp.where((span == 1 << l) & (me // (2 << l) % 2 == 1), 2 << l, 0) for l in range(height) if not upper[l])
    source = top - far

    loads = [pltpu.make_async_copy(a, b, sin.at[i]) for i, (a, b) in enumerate([(s_hbm, s_in), (w_hbm, w_in), (g_hbm, g_in)])]
    for load in loads:
        load.start()
    barrier = pltpu.get_barrier_semaphore()
    for l in range(height):
        @pl.when(left[l])
        def _():
            pl.semaphore_signal(barrier, inc=1, device_id=(me + (2 << l) - 1,), device_id_type=MESH)
            pl.semaphore_signal(barrier, inc=1, device_id=(me + (1 << l),), device_id_type=MESH)
    @pl.when(rest)
    def _():
        pl.semaphore_signal(barrier, inc=1, device_id=(source,), device_id_type=MESH)

    loads[0].wait()
    s0 = s_in[...]
    eye = iota((R, R), 0) == iota((R, R), 1)
    diag = jnp.where(eye, s0, 0.0)
    drow = jnp.sum(diag, axis=0, keepdims=True)
    scol = lax.rsqrt(jnp.sum(diag, axis=1, keepdims=True))
    srow = lax.rsqrt(drow)
    S[...] = s0 * scol * srow
    loads[1].wait()
    W[...] = w_in[...] * scol
    loads[2].wait()
    CG[:, R:] = g_in[...] * scol
    zero_ref[...] = jnp.zeros_like(zero_ref)
    WB[height] = jnp.zeros((R, R), F32)
    for ref in (F, E, RC, L3):
        ref[...] = jnp.zeros_like(ref)
    ld_acc[...] = jnp.broadcast_to(jnp.sum(jnp.log(drow), axis=1, keepdims=True), (8, 128))
    pl.semaphore_wait(barrier, count(single) + count(double) + count(gives) + rest.astype(jnp.int32))

    def send_state(level, target):
        for i, part in enumerate(s_parts):
            Sx[part] = S[part]
            copy_to(Sx.at[part], SB.at[(level,) + part], sS.at[i], rS.at[level, i], target).start()

    def send_rhs(level, target):
        GX[:R, :] = CG[:, R:]
        GX[R:, :] = ld_acc[...]
        copy_to(GX, GB.at[level], sg, rg.at[level], target).start()

    @pl.when(me % 2 != 0)
    def _():
        send_state(0, me - 1)
    for l in range(height):
        @pl.when(gives[l])
        def _():
            copy_to(W, WB.at[l], sw.at[l], rw.at[l], me + 1 - (2 << l)).start()
    @pl.when(me % 2 != 0)
    def _():
        send_rhs(0, me - 1)

    row = iota((B, 128), 0)
    lane = iota((B, 128), 1)

    def finish(slot):
        lb = (R - B) % 128
        ek = mm3(split(L3[...]), split(RC[R - B:, :]), TN)[lb:]
        f = F[:R - B, R - 128:]
        f = jnp.where(iota(f.shape, 1) >= lb, f, 0.0)
        et = jnp.concatenate([E[:R - B, :] - mm3(split(f), split(jnp.concatenate([jnp.zeros_like(ek), ek], 0)), NN), ek], 0)
        Eh[slot], El[slot] = split(et[:, :R].T)
        DT[slot] = et[:, R:].T

    def level(it, st):
        last = it == height

        @pl.when(me % (2 * st) == 0)
        def _():
            @pl.when(jnp.logical_not(last))
            def _():
                copy_to(W, WB.at[it], sw.at[0], rw.at[it], me).wait_recv()
            finish(it)
            for k in range(nk):
                lb = (B * k) % 128
                base = B * k - lb
                lo = B * (k + 1)
                rows, pair = slice(B * k, lo), slice(base, base + 128)
                def eliminate():
                    tiles = [S[rows, t:t + 128] for t in range(base, R, 128)]
                    def put(ti, j, val):
                        if ti is None:
                            r0 = (rows.start + j) // 2
                            det[r0:r0 + 1, :] = val[0][0:1]
                            det[r0 + 1:r0 + 2, :] = val[1][0:1]
                        else:
                            Rs[rows.start + j:rows.start + j + G, base + 128 * ti:base + 128 * ti + 128] = val
                    tiles = sweep(tiles, 0, lb, G, zero_ref[...], put)
                    for i, t in enumerate(tiles):
                        S[rows, base + 128 * i:base + 128 * i + 128] = t
                eliminate()
                Z = S[rows, base:]
                zs = split(Z)
                if k < nk - 1:
                    upd = mm3(zs, split(Rs[rows, base:]), TN)
                    S[lo:, base:] -= upd[lo - base:]
                if k == 0:
                    wb = WB[it]
                    CG[:, :R] = 0.5 * mm3(split(W[...]), split(wb), NT)
                rel = lane - lb
                inside = (rel >= 0) & (rel < B)
                Lk = jnp.where(inside & (rel < G * (row // G)), Z[:, :128], jnp.where(rel == row, 1.0, 0.0))
                DLk = jnp.where(inside & (rel < G * (row // G) + G), Rs[rows, pair], 0.0)
                both = mm3(split(jnp.concatenate([Lk, DLk], 0)), split(CG[pair, :]), NN)
                ZC[rows, :] = both[:B, :R]
                rc = both[B:]
                RC[rows, :] = rc
                ls = split(Lk)
                if k < nk - 1:
                    upd = mm3(zs, split(rc), TN)
                    CG[lo:, :] -= upd[lo - base:]
                    rs = Rs[rows, base:]
                    rs = jnp.where(iota(rs.shape, 1) >= lo - base, rs, 0.0)
                    ft = mm3(ls, split(rs), TN)[lb:lb + B]
                    F[rows, base:] = ft
                    ek = mm3(ls, split(rc), TN)[lb:lb + B]
                    E[rows, :] = ek
                    if k:
                        f = jnp.where((iota((B * k, 128), 1) >= lb) & (iota((B * k, 128), 1) < lb + B), F[:B * k, pair], 0.0)
                        gap = jnp.zeros_like
                        pad = (lambda v: jnp.concatenate([v, gap(v)], 0)) if lb == 0 else (lambda v: jnp.concatenate([gap(v), v], 0))
                        fs = split(f)
                        E[:B * k, :] -= mm3(fs, split(pad(ek)), NN)
                        F[:B * k, base:] -= mm3(fs, split(pad(ft)), NN)
                if k == nk - 2:
                    zc, rr = split(ZC[:lo, :]), split(RC[:lo, :])
                    Uo[:H, :] = mm3([a[:, :H] for a in zc], rr, TN)
                    Uo[H:, H:] = mm3([a[:, H:] for a in zc], [a[:, H:] for a in rr], TN)

            L3[...] = Lk
            zc, rr = split(ZC[rows, :]), split(rc)
            Uo[:H, :] += mm3([a[:, :H] for a in zc], rr, TN)
            Uo[H:, H:] += mm3([a[:, H:] for a in zc], [a[:, H:] for a in rr], TN)
            ld_acc[...] += jnp.broadcast_to(jnp.sum(jnp.log(det[...]), axis=0, keepdims=True), (8, 128))

            @pl.when(jnp.logical_not(last))
            def _():
                for i, part in enumerate(s_parts):
                    copy_to(Sx.at[part], SB.at[(it,) + part], sS.at[i], rS.at[it, i], me).wait_recv()
                S[:H, :] = SB[it, :H, :] - Uo[:H, :R]
                S[H:, H:] = SB[it, H:, H:] - Uo[H:, H:R]
                turn = me % (4 * st) != 0
                @pl.when(turn)
                def _():
                    send_state(it + 1, top)
                copy_to(GX, GB.at[it], sg, rg.at[it], me).wait_recv()
                CG[:H, R:] = GB[it, :H] - Uo[:H, R:]
                CG[H:, R:] = GB[it, H:R] - Uo[H:, R:]
                ld_acc[...] += GB[it, R:]
                @pl.when(turn)
                def _():
                    send_rhs(it + 1, top)
                W[...] = WB[it]
        return st * 2

    lax.fori_loop(0, height + 1, level, jnp.int32(1))

    @pl.when(me % 2 == 0)
    def _():
        finish(count(left) + 1 - rest.astype(jnp.int32))

    @pl.when(jnp.logical_not(rest))
    def _():
        Y[height, :M, :] = DT[height + 1]
        Y[height, M:, :] = jnp.broadcast_to(ld_acc[0:1, 0:1] / (R * n), (8, R))

    def down(i, st):
        it = height - 1 - i

        @pl.when(me % (2 * st) == 0)
        def _():
            high = i % 2 == 0
            for c in range(NC):
                part = Y.at[it + 1, y_parts[c]]
                @pl.when(rest & (span == 2 * st))
                def _():
                    copy_to(part, part, sx.at[it, c], rx.at[c], me).wait_recv()
                @pl.when(high | (me % (4 * st) == 0))
                def _():
                    copy_to(part, Y.at[it, y_parts[c]], sx.at[it, c], rx.at[c], me + st).start()
                @pl.when(high & (it > 0))
                def _():
                    copy_to(part, Y.at[it - 1, y_parts[c]], sx2.at[it, c], rx.at[c], me + st + st // 2).start()
            for c in range(NC):
                r = slice(C * c, C * c + C)
                ah, al = split(Y[it + 1, r, :])
                dg = lambda a, b: jnp.dot(a, b, preferred_element_type=F32)
                Y[it, r, :] = DT[it + 1, r, :] - (dg(ah, Eh[it + 1]) + (dg(al, Eh[it + 1]) + dg(ah, El[it + 1])))
            Y[it, M:, :] = Y[it + 1, M:, :]
        return st // 2

    lax.fori_loop(0, height, down, jnp.int32(n // 2))

    @pl.when(me % 2 != 0)
    def _():
        for c in range(NC):
            copy_to(Y.at[0, y_parts[c]], Y.at[0, y_parts[c]], sx.at[0, c], rx.at[c], source).wait_recv()
    x_out[...] = (Y[0, :M, :] * srow).T
    ld_out[...] = Y[0, M:M + 1, 0:1]
    for l in range(height):
        @pl.when(gives[l])
        def _():
            copy_to(W, WB.at[l], sw.at[l], rw.at[l], me + 1 - (2 << l)).wait_send()
        @pl.when(single[l])
        def _():
            for c in range(NC):
                copy_to(Y.at[0, y_parts[c]], Y.at[0, y_parts[c]], sx.at[l, c], rx.at[c], me + (1 << l)).wait_send()
        @pl.when(double[l])
        def _():
            for c in range(NC):
                copy_to(Y.at[0, y_parts[c]], Y.at[0, y_parts[c]], sx2.at[l, c], rx.at[c], me + (1 << l)).wait_send()
    @pl.when(rest)
    def _():
        for i, part in enumerate(s_parts):
            copy_to(Sx.at[part], SB.at[(0,) + part], sS.at[i], rS.at[0, i], top).wait_send()
        copy_to(GX, GB.at[0], sg, rg.at[0], top).wait_send()


def local(n, blocks, generators, rhs_blocks):
    R, M = rhs_blocks.shape
    height = n.bit_length() - 1
    dma = pltpu.SemaphoreType.DMA
    vm = lambda *s: pltpu.VMEM(s, F32)
    half = pltpu.VMEM((height + 2, R, R), B16)
    x, ld = pl.pallas_call(
        functools.partial(kernel, n),
        out_shape=(jax.ShapeDtypeStruct((R, M), F32), jax.ShapeDtypeStruct((1, 1), F32)),
        in_specs=[pl.BlockSpec(memory_space=pl.ANY)] * 3,
        out_specs=[pl.BlockSpec(memory_space=pltpu.VMEM)] * 2,
        scratch_shapes=[
            vm(R, R), vm(R, R), vm(R, M), vm(R, R), vm(R, R), vm(R, R), vm(height + 1, R, R), vm(height, R, R), vm(height, R + 8, M),
            vm(R + 8, M), vm(R, R + M), vm(R, R + M), vm(R, R), vm(R, R), vm(R, R), vm(R, R + M), vm(B, 128), vm(R, R + M), half, half,
            vm(height + 2, M, R), vm(height + 1, M + 8, R), vm(R // 2, 128), vm(8, 128), vm(G, 128),
            dma((3,)), dma((height,)), dma((height,)), dma((2,)), dma((height, 2)), dma, dma((height,)), dma((height, NC)), dma((height, NC)), dma((NC,)),
        ],
        compiler_params=pltpu.CompilerParams(
            collective_id=0, has_side_effects=True, vmem_limit_bytes=60 * 1024 * 1024
        ),
        name="ulv",
    )(blocks, generators, rhs_blocks)
    return x, ld.reshape(())


def solution(mesh):
    n = mesh.shape["leaf"]
    return jax.shard_map(
        functools.partial(local, n),
        mesh=mesh,
        in_specs=(P("leaf", None), P("leaf", None), P("leaf", None)),
        out_specs=(P("leaf", None), P()),
        check_vma=False,
    )
```

```python
import functools

import jax
import jax.numpy as jnp
from jax import lax
from jax.experimental import pallas as pl
from jax.experimental.pallas import tpu as pltpu
from jax.sharding import PartitionSpec as P

F32 = jnp.float32
B16 = jnp.bfloat16
MESH = pl.DeviceIdType.MESH
G = 8
B = 64
NC = 2

def iota(shape, dim): return lax.broadcasted_iota(jnp.int32, shape, dim)

def sweep(tiles, pt, l, G, zero, put):
    b = tiles[0].shape[0]
    spread = lambda r, c0: [jnp.broadcast_to(tiles[pt][r:r + G, c0+t:c0+t+1], (G, 128)) for t in range(G)]
    c = None
    for j in range(0, b, G):
        if c is None:
            c = [x + zero for x in spread(j, l + j)]
        ahead = later = None
        if j + G < b:
            ahead, later = spread(j + G, l + j), spread(j + G, l + j + G)
        tiles, c = half(tiles, pt, j, l + j, G, c, ahead, later, zero, put)
    return tiles


def half(tiles, pt, j, l, G, c, ahead, later, zero, put):
    b = tiles[0].shape[0]
    T = tiles[pt]
    D = [X[j:j+G] for X in tiles]
    low = [jnp.broadcast_to(T[j+G:, l+t:l+t+1], (b-j-G, 128)) for t in range(G)] if j+G < b else None
    lane = iota((8, 128), 1); sub = iota((G, 128), 0)
    if ahead is not None:
        A = [x + zero for x in ahead]
        V = list(A)
    for q in range(0, G, 4):
        p = lambda s, t: jnp.broadcast_to(c[q+t][q+s:q+s+1], (8, 128))
        a, bb, d = p(0,0), p(0,1), p(1,1)
        e, f, g, h = p(0,2), p(0,3), p(1,2), p(1,3)
        m, n, o = p(2,2), p(2,3), p(3,3)
        det1 = a*d - bb*bb
        i1 = 1.0/det1
        t00, t01 = d*e - bb*g, d*f - bb*h
        t10, t11 = a*g - bb*e, a*h - bb*f
        m2 = m - i1*(e*t00 + g*t10)
        n2 = n - i1*(e*t01 + g*t11)
        o2 = o - i1*(f*t01 + h*t11)
        det2 = m2*o2 - n2*n2
        i2 = 1.0/det2
        u00, u01, u10, u11 = i1*t00, i1*t01, i1*t10, i1*t11
        ia, ib, id_ = i1*a, i1*bb, i1*d
        ja, jb, jd = i2*m2, i2*n2, i2*o2
        put(None, j+q, (det1, det2))
        cs = lambda u, t, c=c: jnp.broadcast_to(c[t][u:u+1], (8, 128))
        def solve(r):
            y0, y1 = id_*r[0] - ib*r[1], ia*r[1] - ib*r[0]
            z2 = r[2] - (e*y0 + g*y1)
            z3 = r[3] - (f*y0 + h*y1)
            w2 = jd*z2 - jb*z3
            w3 = ja*z3 - jb*z2
            w0 = (y0 - u01*w3) - u00*w2
            w1 = (y1 - u11*w3) - u10*w2
            return [w0, w1, w2, w3]
        def apply(X, piv):
            r = [jnp.broadcast_to(X[q+t:q+t+1], (8, 128)) for t in range(4)]
            if piv:
                inp = (lane >= l+q) & (lane < l+q+4)
                r = [jnp.where(inp, jnp.where(lane == l+q+t, 1.0, 0.0), r[t]) for t in range(4)]
            W = solve(r)
            w0, w1, w2, w3 = W
            out = []
            for v in range(G//8):
                xv = X[8*v:8*v+8]
                if piv: xv = jnp.where(inp, 0.0, xv)
                cv = [c[q+t][8*v:8*v+8] for t in range(4)]
                nv = (xv - (cv[2]*w2 + cv[3]*w3)) - (cv[0]*w0 + cv[1]*w1)
                if q//8 == v:
                    for t in range(4): nv = jnp.where(sub[:8] == q%8+t, W[t], nv)
                out.append(nv)
            return jnp.concatenate(out, 0) if len(out) > 1 else out[0]
        nc = list(c)
        if q + 4 < G:
            W = solve([c[q+t] for t in range(4)])
            for t in range(q+4, G):
                w = [jnp.broadcast_to(x[t:t+1], (8, 128)) for x in W]
                nv = (c[t] - (c[q+2]*w[2] + c[q+3]*w[3])) - (c[q]*w[0] + c[q+1]*w[1])
                for u in range(4): nv = jnp.where(sub[:8] == q+u, w[u], nv)
                nc[t] = nv
        if ahead is not None:
            W = solve(V[q:q+4])
            for u in range(G):
                if not q <= u < q + 4:
                    V[u] = (V[u] - (cs(u, q+2)*W[2] + cs(u, q+3)*W[3])) - (cs(u, q)*W[0] + cs(u, q+1)*W[1])
            V[q:q+4] = W
        D = [apply(D[i], i == pt) for i in range(len(tiles))]
        c = nc
    out = []
    if ahead is not None:
        fresh = []
        for t in range(G):
            acc = [None]*4
            for u in range(G):
                pr = A[u]*jnp.broadcast_to(V[u][t:t+1], (8, 128))
                acc[u % 4] = pr if acc[u % 4] is None else acc[u % 4] + pr
            fresh.append((later[t] + zero) - ((acc[0]+acc[1]) + (acc[2]+acc[3])))
        later = fresh
    inpG = (lane >= l) & (lane < l+G)
    for ti, X in enumerate(tiles):
        put(ti, j, D[ti])
        vs = [X[:j+G]]
        if j+G < b:
            R = [jnp.broadcast_to(D[ti][t:t+1], (8, 128)) for t in range(G)]
            for v in range(G//8, (b-j)//8):
                xv = X[j+8*v:j+8*v+8]
                if ti == pt: xv = jnp.where(inpG, 0.0, xv)
                acc = [None]*4
                for t in range(G):
                    pr = low[t][8*(v-G//8):8*(v-G//8)+8]*R[t]
                    k = t % 4
                    acc[k] = pr if acc[k] is None else acc[k] + pr
                vs.append(xv - ((acc[0]+acc[1]) + (acc[2]+acc[3])))
        out.append(jnp.concatenate(vs, 0) if len(vs) > 1 else vs[0])
    return out, later

def split(x):
    hi = x.astype(B16); return hi, (x - hi.astype(F32)).astype(B16)
def mm3(a, b, dn):
    (ah, al), (bh, bl) = a, b
    dg = lambda u, v: lax.dot_general(u, v, dn, preferred_element_type=F32)
    return dg(ah, bh) + (dg(ah, bl) + dg(al, bh))
NN = (((1,), (0,)), ((), ()))
TN = (((0,), (0,)), ((), ()))
NT = (((1,), (1,)), ((), ()))


def copy_to(src, dst, send, recv, device):
    return pltpu.make_async_remote_copy(
        src_ref=src, dst_ref=dst, send_sem=send, recv_sem=recv, device_id=(device,), device_id_type=MESH
    )


def kernel(n, s_hbm, w_hbm, g_hbm, x_out, ld_out, s_in, w_in, g_in, S, Sx, W, WB, SB, GB, GX, Uo, CG, Rs, F, ZC, RC, L3, E, Eh, El, DT, Y,
           det, ld_acc, zero_ref, sin, sw, rw, sS, rS, sg, rg, sx, sx2, rx):
    height = n.bit_length() - 1
    me = lax.axis_index("leaf")
    R, M = g_hbm.shape
    nk = R // B
    H = R // 2
    C = M // NC
    s_parts = [(slice(0, B), slice(0, R)), (slice(B, H), slice(0, R)), (slice(H, R), slice(H, R))]
    y_parts = [slice(C * c, C * c + C + (8 if c == NC - 1 else 0)) for c in range(NC)]
    left = [me % (2 << l) == 0 for l in range(height)]
    gives = [(me + 1) % (2 << l) == 0 for l in range(height)]
    rest = me != 0
    count = lambda flags: sum(f.astype(jnp.int32) for f in flags)
    span = 1 + sum(jnp.where(left[l], 1 << l, 0) for l in range(height))
    top = me - span
    upper = [(height - 1 - l) % 2 == 0 for l in range(height)]
    skips = [(l > 0) and upper[l] for l in range(height)]
    single = [left[l] if upper[l] else (me % (4 << l) == 0) for l in range(height)]
    double = [left[l] if skips[l] else (me % 2 > 1) for l in range(height)]
    far = sum(jnp.where((span == 1 << l) & (me // (2 << l) % 2 == 1), 2 << l, 0) for l in range(height) if not upper[l])
    source = top - far

    loads = [pltpu.make_async_copy(a, b, sin.at[i]) for i, (a, b) in enumerate([(s_hbm, s_in), (w_hbm, w_in), (g_hbm, g_in)])]
    for load in loads:
        load.start()
    barrier = pltpu.get_barrier_semaphore()
    for l in range(height):
        @pl.when(left[l])
        def _():
            pl.semaphore_signal(barrier, inc=1, device_id=(me + (2 << l) - 1,), device_id_type=MESH)
            pl.semaphore_signal(barrier, inc=1, device_id=(me + (1 << l),), device_id_type=MESH)
    @pl.when(rest)
    def _():
        pl.semaphore_signal(barrier, inc=1, device_id=(source,), device_id_type=MESH)

    loads[0].wait()
    s0 = s_in[...]
    eye = iota((R, R), 0) == iota((R, R), 1)
    diag = jnp.where(eye, s0, 0.0)
    drow = jnp.sum(diag, axis=0, keepdims=True)
    scol = lax.rsqrt(jnp.sum(diag, axis=1, keepdims=True))
    srow = lax.rsqrt(drow)
    S[...] = s0 * scol * srow
    loads[1].wait()
    W[...] = w_in[...] * scol
    loads[2].wait()
    CG[:, R:] = g_in[...] * scol
    zero_ref[...] = jnp.zeros_like(zero_ref)
    WB[height] = jnp.zeros((R, R), F32)
    for ref in (F, E, RC, L3):
        ref[...] = jnp.zeros_like(ref)
    ld_acc[...] = jnp.broadcast_to(jnp.sum(jnp.log(drow), axis=1, keepdims=True), (8, 128))
    pl.semaphore_wait(barrier, count(single) + count(double) + count(gives) + rest.astype(jnp.int32))

    def send_state(level, target):
        for i, part in enumerate(s_parts):
            Sx[part] = S[part]
            copy_to(Sx.at[part], SB.at[(level,) + part], sS.at[i], rS.at[level, i], target).start()

    def send_rhs(level, target):
        GX[:R, :] = CG[:, R:]
        GX[R:, :] = ld_acc[...]
        copy_to(GX, GB.at[level], sg, rg.at[level], target).start()

    @pl.when(me % 2 != 0)
    def _():
        send_state(0, me - 1)
    for l in range(height):
        @pl.when(gives[l])
        def _():
            copy_to(W, WB.at[l], sw.at[l], rw.at[l], me + 1 - (2 << l)).start()
    @pl.when(me % 2 != 0)
    def _():
        send_rhs(0, me - 1)

    row = iota((B, 128), 0)
    lane = iota((B, 128), 1)

    def finish(slot):
        lb = (R - B) % 128
        ek = mm3(split(L3[...]), split(RC[R - B:, :]), TN)[lb:]
        f = F[:R - B, R - 128:]
        f = jnp.where(iota(f.shape, 1) >= lb, f, 0.0)
        et = jnp.concatenate([E[:R - B, :] - mm3(split(f), split(jnp.concatenate([jnp.zeros_like(ek), ek], 0)), NN), ek], 0)
        Eh[slot], El[slot] = split(et[:, :R].T)
        DT[slot] = et[:, R:].T

    def take(l, i):
        part = s_parts[i]
        copy_to(Sx.at[part], SB.at[(l,) + part], sS.at[i], rS.at[l, i], me).wait_recv()
        S[part] = SB[(l,) + part] - Uo[part]

    def take_rest(l):
        take(l, 1)
        take(l, 2)
        copy_to(GX, GB.at[l], sg, rg.at[l], me).wait_recv()
        CG[:, R:] = GB[l, :R] - Uo[:, R:]
        ld_acc[...] += GB[l, R:]

    def level(it, st):
        last = it == height

        @pl.when(me % (2 * st) == 0)
        def _():
            @pl.when(jnp.logical_not(last))
            def _():
                copy_to(W, WB.at[it], sw.at[0], rw.at[it], me).wait_recv()
            finish(it)
            for k in range(nk):
                lb = (B * k) % 128
                base = B * k - lb
                lo = B * (k + 1)
                rows, pair = slice(B * k, lo), slice(base, base + 128)
                def eliminate():
                    tiles = [S[rows, t:t + 128] for t in range(base, R, 128)]
                    def put(ti, j, val):
                        if ti is None:
                            r0 = (rows.start + j) // 2
                            det[r0:r0 + 1, :] = val[0][0:1]
                            det[r0 + 1:r0 + 2, :] = val[1][0:1]
                        else:
                            Rs[rows.start + j:rows.start + j + G, base + 128 * ti:base + 128 * ti + 128] = val
                    tiles = sweep(tiles, 0, lb, G, zero_ref[...], put)
                    for i, t in enumerate(tiles):
                        S[rows, base + 128 * i:base + 128 * i + 128] = t
                eliminate()
                Z = S[rows, base:]
                if k == 0:
                    wb = WB[it]
                    CG[:, :R] = 0.5 * mm3(split(W[...]), split(wb), NT)
                    @pl.when(it > 0)
                    def _():
                        take_rest(it - 1)
                zs = split(Z)
                if k < nk - 1:
                    upd = mm3(zs, split(Rs[rows, base:]), TN)
                    S[lo:, base:] -= upd[lo - base:]
                rel = lane - lb
                inside = (rel >= 0) & (rel < B)
                Lk = jnp.where(inside & (rel < G * (row // G)), Z[:, :128], jnp.where(rel == row, 1.0, 0.0))
                DLk = jnp.where(inside & (rel < G * (row // G) + G), Rs[rows, pair], 0.0)
                both = mm3(split(jnp.concatenate([Lk, DLk], 0)), split(CG[pair, :]), NN)
                ZC[rows, :] = both[:B, :R]
                rc = both[B:]
                RC[rows, :] = rc
                ls = split(Lk)
                if k < nk - 1:
                    upd = mm3(zs, split(rc), TN)
                    CG[lo:, :] -= upd[lo - base:]
                    rs = Rs[rows, base:]
                    rs = jnp.where(iota(rs.shape, 1) >= lo - base, rs, 0.0)
                    ft = mm3(ls, split(rs), TN)[lb:lb + B]
                    F[rows, base:] = ft
                    ek = mm3(ls, split(rc), TN)[lb:lb + B]
                    E[rows, :] = ek
                    if k:
                        f = jnp.where((iota((B * k, 128), 1) >= lb) & (iota((B * k, 128), 1) < lb + B), F[:B * k, pair], 0.0)
                        gap = jnp.zeros_like
                        pad = (lambda v: jnp.concatenate([v, gap(v)], 0)) if lb == 0 else (lambda v: jnp.concatenate([gap(v), v], 0))
                        fs = split(f)
                        E[:B * k, :] -= mm3(fs, split(pad(ek)), NN)
                        F[:B * k, base:] -= mm3(fs, split(pad(ft)), NN)
                if k == nk - 2:
                    zc, rr = split(ZC[:lo, :]), split(RC[:lo, :])
                    Uo[:H, :] = mm3([a[:, :H] for a in zc], rr, TN)
                    Uo[H:, H:] = mm3([a[:, H:] for a in zc], [a[:, H:] for a in rr], TN)

            L3[...] = Lk
            zc, rr = split(ZC[rows, :]), split(rc)
            Uo[:H, :] += mm3([a[:, :H] for a in zc], rr, TN)
            Uo[H:, H:] += mm3([a[:, H:] for a in zc], [a[:, H:] for a in rr], TN)
            ld_acc[...] += jnp.broadcast_to(jnp.sum(jnp.log(det[...]), axis=0, keepdims=True), (8, 128))

            @pl.when(jnp.logical_not(last))
            def _():
                take(it, 0)
                @pl.when(me % (4 * st) != 0)
                def _():
                    take_rest(it)
                    send_state(it + 1, top)
                    send_rhs(it + 1, top)
                W[...] = WB[it]
        return st * 2

    lax.fori_loop(0, height + 1, level, jnp.int32(1))

    @pl.when(me % 2 == 0)
    def _():
        finish(count(left) + 1 - rest.astype(jnp.int32))

    @pl.when(jnp.logical_not(rest))
    def _():
        Y[height, :M, :] = DT[height + 1]
        Y[height, M:, :] = jnp.broadcast_to(ld_acc[0:1, 0:1] / (R * n), (8, R))

    def down(i, st):
        it = height - 1 - i

        @pl.when(me % (2 * st) == 0)
        def _():
            high = i % 2 == 0
            for c in range(NC):
                part = Y.at[it + 1, y_parts[c]]
                @pl.when(rest & (span == 2 * st))
                def _():
                    copy_to(part, part, sx.at[it, c], rx.at[c], me).wait_recv()
                @pl.when(high | (me % (4 * st) == 0))
                def _():
                    copy_to(part, Y.at[it, y_parts[c]], sx.at[it, c], rx.at[c], me + st).start()
                @pl.when(high & (it > 0))
                def _():
                    copy_to(part, Y.at[it - 1, y_parts[c]], sx2.at[it, c], rx.at[c], me + st + st // 2).start()
            for c in range(NC):
                r = slice(C * c, C * c + C)
                ah, al = split(Y[it + 1, r, :])
                dg = lambda a, b: jnp.dot(a, b, preferred_element_type=F32)
                Y[it, r, :] = DT[it + 1, r, :] - (dg(ah, Eh[it + 1]) + (dg(al, Eh[it + 1]) + dg(ah, El[it + 1])))
            Y[it, M:, :] = Y[it + 1, M:, :]
        return st // 2

    lax.fori_loop(0, height, down, jnp.int32(n // 2))

    @pl.when(me % 2 != 0)
    def _():
        for c in range(NC):
            copy_to(Y.at[0, y_parts[c]], Y.at[0, y_parts[c]], sx.at[0, c], rx.at[c], source).wait_recv()
    x_out[...] = (Y[0, :M, :] * srow).T
    ld_out[...] = Y[0, M:M + 1, 0:1]
    for l in range(height):
        @pl.when(gives[l])
        def _():
            copy_to(W, WB.at[l], sw.at[l], rw.at[l], me + 1 - (2 << l)).wait_send()
        @pl.when(single[l])
        def _():
            for c in range(NC):
                copy_to(Y.at[0, y_parts[c]], Y.at[0, y_parts[c]], sx.at[l, c], rx.at[c], me + (1 << l)).wait_send()
        @pl.when(double[l])
        def _():
            for c in range(NC):
                copy_to(Y.at[0, y_parts[c]], Y.at[0, y_parts[c]], sx2.at[l, c], rx.at[c], me + (1 << l)).wait_send()
    @pl.when(rest)
    def _():
        for i, part in enumerate(s_parts):
            copy_to(Sx.at[part], SB.at[(0,) + part], sS.at[i], rS.at[0, i], top).wait_send()
        copy_to(GX, GB.at[0], sg, rg.at[0], top).wait_send()


def local(n, blocks, generators, rhs_blocks):
    R, M = rhs_blocks.shape
    height = n.bit_length() - 1
    dma = pltpu.SemaphoreType.DMA
    vm = lambda *s: pltpu.VMEM(s, F32)
    half = pltpu.VMEM((height + 2, R, R), B16)
    x, ld = pl.pallas_call(
        functools.partial(kernel, n),
        out_shape=(jax.ShapeDtypeStruct((R, M), F32), jax.ShapeDtypeStruct((1, 1), F32)),
        in_specs=[pl.BlockSpec(memory_space=pl.ANY)] * 3,
        out_specs=[pl.BlockSpec(memory_space=pltpu.VMEM)] * 2,
        scratch_shapes=[
            vm(R, R), vm(R, R), vm(R, M), vm(R, R), vm(R, R), vm(R, R), vm(height + 1, R, R), vm(height, R, R), vm(height, R + 8, M),
            vm(R + 8, M), vm(R, R + M), vm(R, R + M), vm(R, R), vm(R, R), vm(R, R), vm(R, R + M), vm(B, 128), vm(R, R + M), half, half,
            vm(height + 2, M, R), vm(height + 1, M + 8, R), vm(R // 2, 128), vm(8, 128), vm(G, 128),
            dma((3,)), dma((height,)), dma((height,)), dma((3,)), dma((height, 3)), dma, dma((height,)), dma((height, NC)), dma((height, NC)), dma((NC,)),
        ],
        compiler_params=pltpu.CompilerParams(
            collective_id=0, has_side_effects=True, vmem_limit_bytes=60 * 1024 * 1024
        ),
        name="ulv",
    )(blocks, generators, rhs_blocks)
    return x, ld.reshape(())


def solution(mesh):
    n = mesh.shape["leaf"]
    return jax.shard_map(
        functools.partial(local, n),
        mesh=mesh,
        in_specs=(P("leaf", None), P("leaf", None), P("leaf", None)),
        out_specs=(P("leaf", None), P()),
        check_vma=False,
    )
```
